256 devices in a mesh: grp: 4 (over y), dev: 64 (over z, x, core).
Axes of the slice: x: 4, y: 4, z: 8, core: 2. Of those that a mesh axis runs over, the one named last changes fastest.
Arguments:
- songs: bfloat16 [1024, 48, 768], P(('grp', 'dev')), may hold values from -4 to 4
- gain: float32 [768], replicated, may hold values from 0.5 to 1.5
- enc_weight: bfloat16 [768, 768], replicated, may hold values from -0.21875 to 0.21875
- score_vec: float32 [768], replicated, may hold values from -4 to 4
- left_local: int32 [32768], P(('grp', 'dev')), may hold values from 0 to 3
- right_song: int32 [32768], P(('grp', 'dev')), may hold values from 0 to 1023, as said below
- clique: int32 [1024], replicated, may hold values from 0 to 2
Outputs:
- grad_feats: float32 [1024, 48, 768], P(('grp', 'dev'))
- grad_weight: float32 [768, 768], replicated
- grad_score: float32 [768], replicated
The draws below stay inside these ranges and needn't reach their ends.
Inputs may be any that keep to these rules, and one draw needn't show every extreme that they name: right_song[p] names a song held by a device whose grp index equals that of the device holding pair p; among the pairs held by one device, the songs held by any one device appear as at most one distinct song.
All inputs are finite; a program needn't handle non-finite values.
Results may differ from the reference program's by a relative error of at most 0.012.
The reference program's roundings to bfloat16 on the way (of `hidden` and `features`) count: a program that leaves them out, or rounds other values in their place, can miss the bound.
Values may be sent and summed in bfloat16 or wider, within the bound.
A program may use at most 128 MiB of HBM per device.

```python
import math
import jax
import jax.numpy as jnp
from jax import lax

D = 768
FR = 48
SONG_DEV = 4
PAIR_DEV = 128
SONGS = 1024
PAIRS = 32768
N_GRP = 4
N_DEV = 64
DEVICES = 256


def draw_songs(key, part):
    key = jax.random.fold_in(key, 5)
    values = jnp.clip(jax.random.normal(key, (SONGS, FR, D), jnp.float32), -4.0, 4.0)
    return values.astype(jnp.bfloat16)


def draw_right_song(key, part):
    key = jax.random.fold_in(key, 11)
    key_rank, key_perm, key_pick = jax.random.split(key, 3)
    rank_draws = jax.random.randint(key_rank, (3, PAIRS), 0, N_DEV)
    popularity = jnp.minimum(jnp.minimum(rank_draws[0], rank_draws[1]), rank_draws[2])

    def shuffle(sub_key):
        return jax.random.permutation(sub_key, N_DEV)
    orders = jax.vmap(shuffle)(jax.random.split(key_perm, N_GRP))
    holder = jnp.arange(PAIRS, dtype=jnp.int32) // PAIR_DEV
    group_index = holder // N_DEV
    owner_slot = orders[group_index, popularity]
    song_picks = jax.random.randint(key_pick, (DEVICES, N_DEV), 0, SONG_DEV)
    local_song = song_picks[holder, owner_slot]
    return ((group_index * N_DEV + owner_slot) * SONG_DEV + local_song).astype(jnp.int32)


def set_ends(values, own_key, least, largest):
    longest = values.shape.index(max(values.shape))
    spots = []
    for shift in (0, 1):
        where = [jax.random.randint(jax.random.fold_in(own_key, axis), (), 0, length) for axis, length in enumerate(values.shape)]
        where[longest] = (where[longest] + shift) % values.shape[longest]
        spots.append(tuple(where))
    return values.at[spots[0]].set(least).at[spots[1]].set(largest)


def gaussian(own_key, shape, width, reach, held_as=jnp.bfloat16):
    return jnp.clip(width * jax.random.normal(own_key, shape, jnp.float32), -reach, reach).astype(held_as)


def setup_inputs(seed: int = 0) -> dict:
    seeds = jax.random.split(jax.random.key(seed), 8)
    songs = draw_songs(jax.random.fold_in(seeds[7], 71), 0)
    gain = jnp.clip(1.0 + 0.1 * jax.random.normal(seeds[1], (D,), jnp.float32), 0.5, 1.5)
    enc_weight = gaussian(seeds[2], (D, D), D ** -0.5, 0.21875)
    score_vec = gaussian(seeds[3], (D,), 1.0, 4.0, jnp.float32)
    left_local = set_ends(jax.random.randint(seeds[4], (PAIRS,), 0, SONG_DEV), jax.random.fold_in(seeds[4], 1), 0, SONG_DEV - 1).astype(jnp.int32)
    right_song = draw_right_song(jax.random.fold_in(seeds[7], 71), 0)
    clique = set_ends(jax.random.randint(seeds[6], (SONGS,), 0, 3), jax.random.fold_in(seeds[6], 1), 0, 2).astype(jnp.int32)
    return dict(songs=songs, gain=gain, enc_weight=enc_weight, score_vec=score_vec, left_local=left_local, right_song=right_song, clique=clique)


loss_scale = 16.0

def encode(songs, gain, enc_weight):
    values = songs.astype(jnp.float32)
    square_mean = lax.optimization_barrier(jnp.mean(values * values, axis=-1, keepdims=True))
    hidden = (values * lax.rsqrt(square_mean + 1e-06) * gain).astype(jnp.bfloat16)
    model_width = values.shape[-1]
    projected = jnp.dot(hidden.reshape(-1, model_width), enc_weight, preferred_element_type=jnp.float32)
    features = (values + projected.reshape(values.shape)).astype(jnp.bfloat16)
    return (hidden, features)

def pair_loss(left_values, right_values, score_vec, sign_label):
    left_half = left_values.astype(jnp.bfloat16)
    right_half = right_values.astype(jnp.bfloat16)
    frames = left_half.shape[0]
    model_width = left_half.shape[1]
    scores = jnp.dot(left_half, right_half.T, preferred_element_type=jnp.float32) / math.sqrt(model_width)
    attn_left = jax.nn.softmax(scores, axis=-1).astype(jnp.bfloat16)
    attn_right = jax.nn.softmax(scores.T, axis=-1).astype(jnp.bfloat16)
    out_left = jnp.dot(attn_left, right_half, preferred_element_type=jnp.float32)
    out_right = jnp.dot(attn_right, left_half, preferred_element_type=jnp.float32)
    pooled = (lax.optimization_barrier(jnp.sum(out_left * left_half.astype(jnp.float32), axis=0)) + lax.optimization_barrier(jnp.sum(out_right * right_half.astype(jnp.float32), axis=0))) / math.sqrt(frames)
    logit_value = jnp.sum(pooled * score_vec) / math.sqrt(model_width)
    return loss_scale * jax.nn.softplus(-sign_label * logit_value)

def pair_grads(left_frames, right_frames, score_vec, sign_label):

    def term(left_values, right_values, score_values):
        return pair_loss(left_values, right_values, score_values, sign_label)
    loss_value, pullback = jax.vjp(term, left_frames.astype(jnp.float32), right_frames.astype(jnp.float32), score_vec)
    return pullback(jnp.ones_like(loss_value))

def reference(songs, gain, enc_weight, score_vec, left_local, right_song, clique):
    hidden, features = encode(songs, gain, enc_weight)
    holders = jnp.arange(PAIRS, dtype=jnp.int32) // PAIR_DEV
    left_song = holders * SONG_DEV + left_local
    signs = jnp.where(clique[left_song] == clique[right_song], 1.0, -1.0).astype(jnp.float32)
    batched = jax.vmap(pair_grads, in_axes=(0, 0, None, 0))

    def device_step(totals, device):
        grad_all, score_total = totals
        start = (device * PAIR_DEV).astype(jnp.int32)
        lefts = lax.dynamic_slice_in_dim(left_song, start, PAIR_DEV)
        rights = lax.dynamic_slice_in_dim(right_song, start, PAIR_DEV)
        sign_block = lax.dynamic_slice_in_dim(signs, start, PAIR_DEV)
        grad_left, grad_right, grad_score = batched(features[lefts], features[rights], score_vec, sign_block)
        grad_all = grad_all.at[lefts].add(grad_left).at[rights].add(grad_right)
        return ((grad_all, score_total + lax.optimization_barrier(jnp.sum(grad_score, axis=0))), None)
    start_totals = (jnp.zeros((SONGS, FR, D), jnp.float32), jnp.zeros((D,), jnp.float32))
    (grad_feats, grad_score), _ = lax.scan(device_step, start_totals, jnp.arange(DEVICES, dtype=jnp.int32))
    grad_weight = jnp.dot(hidden.reshape(-1, D).astype(jnp.float32).T, grad_feats.reshape(-1, D), precision=lax.Precision.HIGHEST)
    return (grad_feats, grad_weight, grad_score)
```

```python
import functools
import math

import jax
import jax.numpy as jnp
from jax import lax
from jax.experimental import pallas as pl
from jax.experimental.pallas import tpu as pltpu
from jax.sharding import PartitionSpec as P

D = 768
FR = 48
OWN = 4 * FR
UNIT = 2 * FR
BLK = D // 128
UROWS = UNIT * BLK + 16
LANES = 8 * FR
RING = 32
NB = 32
LOSS_SCALE = 16.0
LOG2E = math.log2(math.e)
C0 = 1.0 / (math.sqrt(FR) * math.sqrt(D))
F32 = jnp.float32
BF16 = jnp.bfloat16
MESH = pl.DeviceIdType.MESH


def ring_pos(z, x):
    u = (z - 3 * x + 24) % 8
    return (4 * z + (x + z) % 4, 4 * x + 16 * (u // 4) + u % 4)


def ring_chip(k, i):
    if k == 0:
        z = i // 4
        return z * 4 + (i % 4 - z + 8) % 4
    j = i // 4
    return ((3 * j + i % 4) % 8) * 4 + j % 4


def dot_nn(a, b):
    return jnp.dot(a, b, preferred_element_type=F32)


def dot_nt(a, b):
    return lax.dot_general(a, b, (((1,), (1,)), ((), ())), preferred_element_type=F32)


def dot_tn(a, b):
    return lax.dot_general(a, b, (((0,), (0,)), ((), ())), preferred_element_type=F32)


def col_softmax(scores):
    scale = LOG2E / math.sqrt(D)
    top = jnp.max(scores, axis=0, keepdims=True)
    e = jnp.exp2((scores - top) * scale)
    return e * (1.0 / jnp.sum(e, axis=0, keepdims=True))


def batch_terms(peer, own_t, own_st, seg, weights, signs):
    scores_x = dot_nn(peer, own_t)
    by_peer = jnp.concatenate(
        [col_softmax(scores_x[p * FR : (p + 1) * FR]) for p in range(8)], axis=0
    )
    by_peer = by_peer.T[:OWN].astype(BF16)
    both = dot_nt(own_st, peer)
    total, first, second, z1s = [], [], [], []
    for a in range(4):
        rows = slice(a * FR, (a + 1) * FR)
        t = both[OWN + a * FR : OWN + (a + 1) * FR]
        p1 = by_peer[rows].astype(F32)
        p2 = col_softmax(both[rows]).astype(BF16).astype(F32)
        z1 = p1 * t
        z2 = p2 * t
        r2 = jnp.sum(z2, axis=0, keepdims=True)
        total.append(jnp.sum(z1, axis=0, keepdims=True) + r2)
        z1s.append(z1.astype(BF16))
        first.append(p1 + p2)
        second.append((z1 + z2 - p2 * r2, p1))
    sums = jnp.concatenate(total + [jnp.zeros((4, LANES), F32)], axis=0)
    high = sums.astype(BF16)
    low = (sums - high.astype(F32)).astype(BF16)
    spread = dot_nn(jnp.concatenate([high, low], axis=0), seg)
    logit = (spread[:8] + spread[8:]) * C0
    coef = weights * signs * (-LOSS_SCALE * C0) / (1.0 + jnp.exp(signs * logit))
    r1 = dot_nn(jnp.concatenate(z1s, axis=0), seg)
    out1, out2 = [], []
    for a in range(4):
        c = coef[a : a + 1]
        g, p1 = second[a]
        out1.append((c * first[a]).astype(BF16))
        out2.append((c * (g - p1 * r1[a * FR : (a + 1) * FR])).astype(BF16))
    return jnp.concatenate(out1 + out2, axis=0)


def pair_kernel(
    x_ref, gain_ref, w_ref, v_ref, meta_ref, ws_ref,
    gf_ref, hid_ref, gs_ref,
    buf, own_st, own_t, seg, ind8, ind_m, sel, acc, ssem, rsem,
):
    grp = lax.axis_index("grp")
    me = lax.axis_index("dev")
    core = me % 2
    chip = me // 2
    sib = me + 1 - 2 * core
    pos = ring_pos(chip // 4, chip % 4)
    near = [
        [ring_chip(k, (pos[k] + step) % RING) * 2 + core for k in range(2)]
        for step in (1, RING - 1)
    ]

    barrier = pltpu.get_barrier_semaphore()
    for dev in near[0] + near[1] + [sib]:
        pl.semaphore_signal(barrier, inc=1, device_id=(grp, dev), device_id_type=MESH)

    def remote(sb, su, db, du, dev):
        return pltpu.make_async_remote_copy(
            src_ref=buf.at[sb, su],
            dst_ref=buf.at[db, du],
            send_sem=ssem.at[db, du],
            recv_sem=rsem.at[db, du],
            device_id=(grp, dev),
            device_id_type=MESH,
        )

    def arrived(b, u):
        remote(b, u, b, u, sib).wait_recv()

    values = x_ref[...].astype(F32)
    square_mean = jnp.mean(values * values, axis=-1, keepdims=True)
    hidden = (values * lax.rsqrt(square_mean + 1e-06) * gain_ref[...]).astype(BF16)
    hid_ref[...] = hidden
    feats = (values + dot_nn(hidden, w_ref[...])).astype(BF16)
    for k in range(2):
        for j in range(BLK):
            buf[0, k, j * UNIT : (j + 1) * UNIT, :] = feats[
                k * UNIT : (k + 1) * UNIT, j * 128 : (j + 1) * 128
            ]
        buf[0, k, BLK * UNIT : UROWS, :] = meta_ref[k]

    pl.semaphore_wait(barrier, 5)
    for k in range(2):
        remote(0, k, 0, 2 + k, sib).start()
        for way in range(2):
            remote(0, k, 1, way * 2 + k, near[way][k]).start()

    own_st[:OWN] = feats
    scaled = (feats.astype(F32) * v_ref[...]).astype(BF16)
    own_st[OWN:] = scaled
    own_t[...] = jnp.concatenate(
        [feats, jnp.zeros((256 - OWN, D), BF16)], axis=0
    ).T

    def ids(shape, dim):
        return lax.broadcasted_iota(jnp.int32, shape, dim)

    def mark(cond):
        return jnp.where(cond, 1.0, 0.0).astype(BF16)

    shape = (LANES, LANES)
    seg[...] = mark(ids(shape, 0) // FR == ids(shape, 1) // FR)
    shape = (128, LANES)
    ind8[...] = mark(ids(shape, 0) == ids(shape, 1) // FR)
    shape = (64, LANES)
    row = ids(shape, 0)
    song = 2 * (row // 16) + (row % 16) // 2
    right_row = jnp.logical_and(row % 16 < 4, row % 2 == me // 32)
    ind_m[...] = mark(jnp.logical_and(right_row, song == ids(shape, 1) // FR))
    shape = (16, 128)
    wanted = jnp.logical_and(ids(shape, 0) < 4, ids(shape, 1) == (me % 32) * 4 + ids(shape, 0))
    sel[...] = mark(wanted)
    acc[...] = jnp.zeros_like(acc)

    def step(b, carry):
        odd = b % 2

        @pl.when(b == 0)
        def _():
            arrived(0, 2)
            arrived(0, 3)

        @pl.when(jnp.logical_and(odd == 1, b < NB - 1))
        def _():
            for u in range(4):
                arrived(b, u)
                if u < 2:
                    remote(b, u, b + 2, u, near[0][u]).start()
                else:

                    @pl.when(b < NB - 3)
                    def _():
                        remote(b, u, b + 2, u, near[1][u - 2]).start()

                remote(b, u, b + 1, u, sib).start()

        @pl.when(jnp.logical_and(odd == 0, b > 0))
        def _():
            for u in range(4):
                arrived(b, u)

        @pl.when(b == NB - 1)
        def _():
            for k in range(2):
                arrived(NB - 1, k)
                remote(NB - 1, k, NB - 1, 2 + k, sib).start()
            for k in range(2):
                arrived(NB - 1, 2 + k)

        peer = jnp.concatenate(
            [
                buf[b, :, j * UNIT : (j + 1) * UNIT, :].reshape(LANES, 128)
                for j in range(BLK)
            ],
            axis=1,
        )
        meta = buf[b, :, BLK * UNIT : UROWS, :].reshape(64, 128)
        wexp = dot_nn(ws_ref[b], ind8[...])
        right = dot_nn(dot_nt(sel[...], meta).astype(BF16), ind_m[...])
        terms = batch_terms(
            peer, own_t[...], own_st[...], seg[...], wexp[:8] + right[:8], wexp[8:]
        )
        acc[...] += dot_nn(terms, peer)
        return carry

    lax.fori_loop(0, NB, step, 0)

    first = acc[:OWN]
    gf_ref[...] = v_ref[...] * first + acc[OWN:] * (1.0 / math.sqrt(D))
    score = 0.5 * jnp.sum(own_st[:OWN].astype(F32) * first, axis=0, keepdims=True)
    gs_ref[...] = jnp.broadcast_to(score, (8, D))

    def drain(b, carry):
        for u in range(4):
            if u < 2:

                @pl.when(b > 0)
                def _():
                    remote(b, u, b, u, sib).wait_send()

            else:
                remote(b, u, b, u, sib).wait_send()
        return carry

    lax.fori_loop(0, NB, drain, 0)


def pair_grads(songs, gain, enc_weight, score_vec, meta, ws):
    vmem = pl.BlockSpec(memory_space=pltpu.VMEM)
    return pl.pallas_call(
        pair_kernel,
        out_shape=(
            jax.ShapeDtypeStruct((OWN, D), F32),
            jax.ShapeDtypeStruct((OWN, D), BF16),
            jax.ShapeDtypeStruct((8, D), F32),
        ),
        in_specs=[vmem] * 6,
        out_specs=(vmem,) * 3,
        scratch_shapes=[
            pltpu.VMEM((NB, 4, UROWS, 128), BF16),
            pltpu.VMEM((2 * OWN, D), BF16),
            pltpu.VMEM((D, 256), BF16),
            pltpu.VMEM((LANES, LANES), BF16),
            pltpu.VMEM((128, LANES), BF16),
            pltpu.VMEM((64, LANES), BF16),
            pltpu.VMEM((16, 128), BF16),
            pltpu.VMEM((2 * OWN, D), F32),
            pltpu.SemaphoreType.DMA((NB, 4)),
            pltpu.SemaphoreType.DMA((NB, 4)),
        ],
        compiler_params=pltpu.CompilerParams(
            collective_id=0, has_side_effects=True, vmem_limit_bytes=52 * 2**20
        ),
    )(songs, gain, enc_weight, score_vec, meta, ws)


FLAT = BLK * D
HALF = FLAT // 2
QUARTER = HALF // 4
PIECE = QUARTER // 4


def reduce_kernel(
    hid_ref, gf_ref, gs_ref,
    out_ref, score_ref,
    flat, rc, sx, rx, sy, ry, rz, full, tc, tx, ty, tz, sems, rems,
):
    y = lax.axis_index("grp")
    me = lax.axis_index("dev")
    core = me % 2
    chip = me // 2
    x = chip % 4
    z = chip // 4
    sib = (y, me + 1 - 2 * core)
    along_x = [(y, (z * 4 + (x + s) % 4) * 2 + core) for s in range(1, 4)]
    along_y = [((y + s) % 4, me) for s in range(1, 4)]
    along_z = [(y, (((z + s) % 8) * 4 + x) * 2 + core) for s in range(1, 8)]

    barrier = pltpu.get_barrier_semaphore()
    for dev in [sib] + along_x + along_y + along_z:
        pl.semaphore_signal(barrier, inc=1, device_id=dev, device_id_type=MESH)

    count = [0]
    pending = []

    def remote(src, dst, dev):
        i = count[0]
        count[0] += 1
        copy = pltpu.make_async_remote_copy(
            src_ref=src, dst_ref=dst, send_sem=sems.at[i], recv_sem=rems.at[i],
            device_id=dev, device_id_type=MESH,
        )
        copy.start()
        pending.append(copy)
        return copy

    def rows(start, size):
        return pl.ds(pl.multiple_of(start, 16), size)

    gf = gf_ref[...]
    high = gf.astype(BF16)
    low = (gf - high.astype(F32)).astype(BF16)
    hidden = hid_ref[...]
    hidden_t = hidden.T
    for j in range(BLK):
        cols = slice(j * 128, (j + 1) * 128)
        part = dot_nn(hidden_t, high[:, cols]) + dot_nn(hidden_t, low[:, cols])
        flat[j * D : (j + 1) * D, :] = part.astype(BF16)
    score = jnp.concatenate(
        [gs_ref[0:1, j * 128 : (j + 1) * 128] for j in range(BLK)]
        + [jnp.zeros((8 - BLK, 128), F32)],
        axis=0,
    )
    pl.semaphore_wait(barrier, 14)

    tc[core] = score
    a = remote(flat.at[rows((1 - core) * HALF, HALF)], rc, sib)
    b = remote(tc.at[core], tc.at[core], sib)
    a.wait_recv()
    b.wait_recv()
    sx[...] = (
        flat[rows(core * HALF, HALF), :].astype(F32) + rc[...].astype(F32)
    ).astype(BF16)
    tx[x] = tc[0] + tc[1]

    copies = []
    for s, dev in enumerate(along_x):
        to = (x + s + 1) % 4
        copies.append(remote(sx.at[rows(to * QUARTER, QUARTER)], rx.at[s], dev))
        copies.append(remote(tx.at[x], tx.at[x], dev))
    for c in copies:
        c.wait_recv()
    sy[...] = (
        sx[rows(x * QUARTER, QUARTER), :].astype(F32)
        + rx[0].astype(F32)
        + rx[1].astype(F32)
        + rx[2].astype(F32)
    ).astype(BF16)
    ty[y] = (tx[0] + tx[1]) + (tx[2] + tx[3])

    copies = []
    for s, dev in enumerate(along_y):
        to = (y + s + 1) % 4
        copies.append(remote(sy.at[rows(to * PIECE, PIECE)], ry.at[s], dev))
        copies.append(remote(ty.at[y], ty.at[y], dev))
    for c in copies:
        c.wait_recv()
    rz[z] = (
        sy[rows(y * PIECE, PIECE), :].astype(F32)
        + ry[0].astype(F32)
        + ry[1].astype(F32)
        + ry[2].astype(F32)
    ).astype(BF16)
    tz[z] = (ty[0] + ty[1]) + (ty[2] + ty[3])

    copies = []
    for dev in along_z:
        copies.append(remote(rz.at[z], rz.at[z], dev))
        copies.append(remote(tz.at[z], tz.at[z], dev))
    for c in copies:
        c.wait_recv()
    total = rz[0].astype(F32)
    score = tz[0]
    for i in range(1, 8):
        total = total + rz[i].astype(F32)
        score = score + tz[i]
    score_ref[...] = score
    first = core * HALF + x * QUARTER
    mine = rows(first + y * PIECE, PIECE)
    full[mine, :] = total.astype(BF16)

    copies = [remote(full.at[mine], full.at[mine], dev) for dev in along_y]
    for c in copies:
        c.wait_recv()
    quarter = rows(first, QUARTER)
    copies = [remote(full.at[quarter], full.at[quarter], dev) for dev in along_x]
    for c in copies:
        c.wait_recv()
    half = rows(core * HALF, HALF)
    remote(full.at[half], full.at[half], sib).wait_recv()
    for j in range(BLK):
        out_ref[:, j * 128 : (j + 1) * 128] = full[j * D : (j + 1) * D, :]
    for c in pending:
        c.wait_send()


def reduce_grads(hidden, grad_feats, score):
    vmem = pl.BlockSpec(memory_space=pltpu.VMEM)
    n_copies = 2 + 6 + 6 + 14 + 3 + 3 + 1
    return pl.pallas_call(
        reduce_kernel,
        out_shape=(
            jax.ShapeDtypeStruct((D, D), BF16),
            jax.ShapeDtypeStruct((8, 128), F32),
        ),
        in_specs=[vmem] * 3,
        out_specs=(vmem,) * 2,
        scratch_shapes=[
            pltpu.VMEM((FLAT, 128), BF16),
            pltpu.VMEM((HALF, 128), BF16),
            pltpu.VMEM((HALF, 128), BF16),
            pltpu.VMEM((3, QUARTER, 128), BF16),
            pltpu.VMEM((QUARTER, 128), BF16),
            pltpu.VMEM((3, PIECE, 128), BF16),
            pltpu.VMEM((8, PIECE, 128), BF16),
            pltpu.VMEM((FLAT, 128), BF16),
            pltpu.VMEM((2, 8, 128), F32),
            pltpu.VMEM((4, 8, 128), F32),
            pltpu.VMEM((4, 8, 128), F32),
            pltpu.VMEM((8, 8, 128), F32),
            pltpu.SemaphoreType.DMA((n_copies,)),
            pltpu.SemaphoreType.DMA((n_copies,)),
        ],
        compiler_params=pltpu.CompilerParams(
            collective_id=1, has_side_effects=True, vmem_limit_bytes=40 * 2**20
        ),
    )(hidden, grad_feats, score)


def batch_songs(me):
    core = me % 2
    chip = me // 2
    pos = ring_pos(chip // 4, chip % 4)
    b = jnp.arange(NB, dtype=jnp.int32)[:, None]
    u = jnp.arange(4, dtype=jnp.int32)[None, :]
    k = u % 2
    ends = jnp.logical_or(b == 0, b == NB - 1)
    t = (b + 1) // 2
    way = jnp.where(jnp.logical_and(u >= 2, jnp.logical_not(ends)), 1, 0)
    at = [(p + jnp.where(way == 1, t, RING - t)) % RING for p in pos]
    origin = jnp.where(k == 0, ring_chip(0, at[0]), ring_chip(1, at[1]))
    other = jnp.where(ends, u // 2, (b + 1) % 2)
    held = origin * 2 + jnp.where(other == 1, 1 - core, core)
    first = held * 4 + 2 * k
    return (first[:, :, None] + jnp.arange(2, dtype=jnp.int32)).reshape(NB, 8)


def pair_tables(left_local, right_rel, clique, group, me):
    hot_left = left_local[None, :] == jnp.arange(4, dtype=jnp.int32)[:, None]
    hot_right = right_rel[:, None] == jnp.arange(256, dtype=jnp.int32)[None, :]
    counts = dot_nn(hot_left.astype(BF16), hot_right.astype(BF16)).astype(BF16)
    meta = counts.reshape(2, 4, 128)
    meta = jnp.pad(meta, ((0, 0), (0, 12), (0, 0)))
    songs = batch_songs(me)
    hot = jnp.arange(256, dtype=jnp.int32)[:, None] == songs.reshape(1, 256)
    own = clique_of(clique, group * 256 + me * 4, 4)
    theirs = clique_of(clique, group * 256, 256)
    signs = jnp.where(own[:, None] == theirs[None, :], 1.0, -1.0).astype(BF16)
    rows = jnp.concatenate([counts, signs], axis=0)
    rows = dot_nn(rows, hot.astype(BF16)).reshape(8, NB, 8)
    rows = rows.transpose(1, 0, 2).astype(BF16)
    ws = jnp.zeros((NB, 16, 128), BF16)
    ws = ws.at[:, 0:4, 0:8].set(rows[:, 0:4]).at[:, 8:12, 0:8].set(rows[:, 4:8])
    return meta, ws


def clique_of(clique, start, size):
    return lax.dynamic_slice_in_dim(clique, start, size)


def local(songs, gain, enc_weight, score_vec, left_local, right_song, clique):
    group = lax.axis_index("grp")
    me = lax.axis_index("dev")
    meta, ws = pair_tables(left_local, right_song - group * 256, clique, group, me)
    gf, hidden, score = pair_grads(
        songs.reshape(OWN, D), gain.reshape(1, D), enc_weight, score_vec.reshape(1, D), meta, ws
    )
    weight, total = reduce_grads(hidden, gf, score)
    return (
        gf.reshape(4, FR, D),
        weight.astype(F32),
        total[:BLK].reshape(D),
    )


def solution(mesh):
    in_specs = (
        P(("grp", "dev"), None, None),
        P(),
        P(),
        P(),
        P(("grp", "dev")),
        P(("grp", "dev")),
        P(),
    )
    out_specs = (P(("grp", "dev"), None, None), P(), P())
    return jax.shard_map(local, mesh=mesh, in_specs=in_specs, out_specs=out_specs, check_vma=False)
```

```python
import functools
import math

import jax
import jax.numpy as jnp
from jax import lax
from jax.experimental import pallas as pl
from jax.experimental.pallas import tpu as pltpu
from jax.sharding import PartitionSpec as P

D = 768
FR = 48
OWN = 4 * FR
OWN2 = 2 * OWN
UNIT = 2 * FR
BLK = D // 128
UROWS = UNIT * BLK + 16
LANES = 8 * FR
RING = 32
NB = 16
SUB = 3
CUTS = (0, 192, 384, 592)
LOSS_SCALE = 16.0
LOG2E = math.log2(math.e)
C0 = 1.0 / (math.sqrt(FR) * math.sqrt(D))
F32 = jnp.float32
BF16 = jnp.bfloat16
MESH = pl.DeviceIdType.MESH


def ring_pos(z, x):
    u = (z - 3 * x + 24) % 8
    return (4 * z + (x + z) % 4, 4 * x + 16 * (u // 4) + u % 4)


def ring_chip(k, i):
    if k == 0:
        z = i // 4
        return z * 4 + (i % 4 - z + 8) % 4
    j = i // 4
    return ((3 * j + i % 4) % 8) * 4 + j % 4


def dot_nn(a, b):
    return jnp.dot(a, b, preferred_element_type=F32)


def dot_nt(a, b):
    return lax.dot_general(a, b, (((1,), (1,)), ((), ())), preferred_element_type=F32)


def dot_tn(a, b):
    return lax.dot_general(a, b, (((0,), (0,)), ((), ())), preferred_element_type=F32)


def col_softmax(scores):
    scale = LOG2E / math.sqrt(D)
    top = jnp.max(scores, axis=0, keepdims=True)
    e = jnp.exp2((scores - top) * scale)
    return e * (1.0 / jnp.sum(e, axis=0, keepdims=True))


def batch_scores(peer, own_t, own_st):
    scores_x = dot_nn(peer, own_t)
    by_peer = jnp.concatenate(
        [col_softmax(scores_x[p * FR : (p + 1) * FR]) for p in range(8)], axis=0
    )
    by_peer = by_peer.T.astype(BF16)
    return by_peer, dot_nt(own_st, peer)


def batch_terms(by_peer, both, seg, weights, signs):
    total, first, second, z1s = [], [], [], []
    for a in range(8):
        rows = slice(a * FR, (a + 1) * FR)
        t = both[OWN2 + a * FR : OWN2 + (a + 1) * FR]
        p1 = by_peer[rows].astype(F32)
        p2 = col_softmax(both[rows]).astype(BF16).astype(F32)
        z1 = p1 * t
        z2 = p2 * t
        r2 = jnp.sum(z2, axis=0, keepdims=True)
        total.append(jnp.sum(z1, axis=0, keepdims=True) + r2)
        z1s.append(z1.astype(BF16))
        first.append(p1 + p2)
        second.append((z1 + z2 - p2 * r2, p1))
    sums = jnp.concatenate(total, axis=0)
    high = sums.astype(BF16)
    low = (sums - high.astype(F32)).astype(BF16)
    spread = dot_nn(jnp.concatenate([high, low], axis=0), seg)
    logit = (spread[:8] + spread[8:]) * C0
    coef = weights * signs * (-LOSS_SCALE * C0) / (1.0 + jnp.exp(signs * logit))
    r1 = dot_nn(jnp.concatenate(z1s, axis=0), seg)
    out1, out2 = [], []
    for a in range(8):
        c = coef[a : a + 1]
        g, p1 = second[a]
        out1.append((c * first[a]).astype(BF16))
        out2.append((c * (g - p1 * r1[a * FR : (a + 1) * FR])).astype(BF16))
    return jnp.concatenate(out1 + out2, axis=0)


FLAT = BLK * D
HALF = FLAT // 2
QUARTER = HALF // 4
PIECE = QUARTER // 4
N_COPIES = 4 + 2 + 6 + 6 + 14 + 3 + 3 + 1


def kernel(
    x_ref, gain_ref, w_ref, v_ref, left_ref, right_ref, clique_ref,
    gf_ref, out_ref, score_ref,
    buf, own8, own_st, own_t, hid, hid_t, cnt, seg, ind_m, sel, small, terms, acc,
    give, got,
    flat, rc, sx, rx, sy, ry, rz, full, tc, tx, ty, tz,
    ssem, rsem, sems, rems,
):
    y = lax.axis_index("grp")
    me = lax.axis_index("dev")
    core = me % 2
    chip = me // 2
    x = chip % 4
    z = chip // 4
    pos = ring_pos(z, x)
    near = [
        [(y, ring_chip(k, (pos[k] + step) % RING) * 2 + core) for k in range(2)]
        for step in (1, RING - 1)
    ]
    sib_dev = me + 1 - 2 * core
    sib = (y, sib_dev)
    along_x = [(y, (z * 4 + (x + s) % 4) * 2 + core) for s in range(1, 4)]
    along_y = [((y + s) % 4, me) for s in range(1, 4)]
    along_z = [(y, (((z + s) % 8) * 4 + x) * 2 + core) for s in range(1, 8)]

    barrier = pltpu.get_barrier_semaphore()
    for dev in [sib] + along_x + along_y + along_z:
        pl.semaphore_signal(barrier, inc=1, device_id=dev, device_id_type=MESH)

    def ring(sb, su, db, du, dev, s):
        part = pl.ds(CUTS[s], CUTS[s + 1] - CUTS[s])
        return pltpu.make_async_remote_copy(
            src_ref=buf.at[sb, su, part],
            dst_ref=buf.at[db, du, part],
            send_sem=ssem.at[db, du * SUB + s],
            recv_sem=rsem.at[db, du * SUB + s],
            device_id=dev,
            device_id_type=MESH,
        )

    count = [0]
    pending = []

    def remote(src, dst, dev):
        i = count[0]
        count[0] += 1
        copy = pltpu.make_async_remote_copy(
            src_ref=src, dst_ref=dst, send_sem=sems.at[i], recv_sem=rems.at[i],
            device_id=dev, device_id_type=MESH,
        )
        copy.start()
        pending.append(copy)
        return copy

    def rows(start, size):
        return pl.ds(pl.multiple_of(start, 16), size)

    def ids(shape, dim):
        return lax.broadcasted_iota(jnp.int32, shape, dim)

    def mark(cond):
        return jnp.where(cond, 1.0, 0.0).astype(BF16)

    values = x_ref[...].astype(F32)
    square_mean = jnp.mean(values * values, axis=-1, keepdims=True)
    hidden = (values * lax.rsqrt(square_mean + 1e-06) * gain_ref[...]).astype(BF16)
    feats = (values + dot_nn(hidden, w_ref[...])).astype(BF16)
    hot_left = mark(ids((16, 128), 0) == left_ref[...])
    hot_right = mark(ids((256, 128), 0) == right_ref[...] - y * 256)
    counts = dot_nt(hot_left, hot_right)
    for k in range(2):
        for j in range(BLK):
            buf[NB - 1, 2 + k, j * UNIT : (j + 1) * UNIT, :] = feats[
                k * UNIT : (k + 1) * UNIT, j * 128 : (j + 1) * 128
            ]
        lines = [
            counts[2 * k + l : 2 * k + l + 1, h * 128 : (h + 1) * 128]
            for l in range(2)
            for h in range(2)
        ]
        buf[NB - 1, 2 + k, BLK * UNIT : UROWS, :] = jnp.concatenate(
            lines + [jnp.zeros((12, 128), F32)], axis=0
        ).astype(BF16)
    own8[:OWN] = feats
    hid[:OWN] = hidden
    cnt[0] = counts.astype(BF16)

    pl.semaphore_wait(barrier, 14)
    for s in range(SUB):
        for k in range(2):
            for way in range(2):
                ring(NB - 1, 2 + k, 0, way * 2 + k, near[way][k], s).start()
    fcopy = remote(own8.at[pl.ds(0, OWN)], own8.at[pl.ds(OWN, OWN)], sib)
    ccopy = remote(cnt.at[0], cnt.at[1], sib)
    hcopy = remote(hid.at[pl.ds(0, OWN)], hid.at[pl.ds(OWN, OWN)], sib)

    shape = (LANES, LANES)
    seg[...] = mark(ids(shape, 0) // FR == ids(shape, 1) // FR)
    shape = (64, LANES)
    row = ids(shape, 0)
    song = 2 * (row // 16) + (row % 16) // 2
    right_row = jnp.logical_and(row % 16 < 4, row % 2 == me // 32)
    ind_m[...] = mark(jnp.logical_and(right_row, song == ids(shape, 1) // FR))
    shape = (16, 128)
    row = ids(shape, 0)
    own_song = jnp.where(row < 4, (me % 32) * 4 + row, (sib_dev % 32) * 4 + row - 4)
    chosen = jnp.logical_and(row < 8, ids(shape, 1) == own_song)
    sel[...] = mark(chosen)
    acc[...] = jnp.zeros_like(acc)
    terms[...] = jnp.zeros_like(terms)

    shape = (256, 128)
    lane = ids((1, 128), 1)
    t = lane // 8 + 1
    u = (lane % 8) // 2
    k = u % 2
    last = jnp.logical_and(t == NB, u >= 2)
    shift = jnp.where(last, 0, jnp.where(u >= 2, t, RING - t))
    origin = jnp.where(
        k == 0, ring_chip(0, (pos[0] + shift) % RING), ring_chip(1, (pos[1] + shift) % RING)
    )
    landing = (origin * 2 + core) * 4 + 2 * k + lane % 2
    hot = mark(ids(shape, 0) == landing)
    group_rows = [clique_ref[pl.ds(2 * y + h, 1), :] for h in range(2)]
    theirs = jnp.concatenate(group_rows, axis=1).astype(F32)
    near_row = clique_ref[pl.ds(2 * y + me // 32, 1), :].astype(F32)
    mine = jnp.sum(jnp.where(chosen, near_row, 0.0), axis=1, keepdims=True)[:8]
    signs = jnp.where(mine == theirs, 1.0, -1.0)
    fcopy.wait_recv()
    ccopy.wait_recv()
    table = jnp.concatenate(
        [cnt[0].astype(F32)[:4], cnt[1].astype(F32)[:4], signs], axis=0
    ).astype(BF16)
    small[...] = dot_nn(table, hot).astype(BF16)
    feats8 = own8[...]
    own_st[:OWN2] = feats8
    own_st[OWN2:] = (feats8.astype(F32) * v_ref[...]).astype(BF16)
    own_t[...] = feats8.T

    def peer_of(b):
        return jnp.concatenate(
            [
                buf[b, :, j * UNIT : (j + 1) * UNIT, :].reshape(LANES, 128)
                for j in range(BLK)
            ],
            axis=1,
        )

    def step(b, carry):
        for s in range(SUB):
            for u in range(4):

                def hop():
                    ring(b, u, b, u, sib, s).wait_recv()
                    way = near[u // 2][u % 2]

                    @pl.when(b < (NB - 1 if u < 2 else NB - 2))
                    def _():
                        ring(b, u, b + 1, u, way, s).start()

                if u < 2:
                    hop()
                else:
                    pl.when(b < NB - 1)(hop)

        peer = peer_of(b)
        by_peer, both = batch_scores(peer, own_t[...], own_st[...])

        acc[...] += dot_nn(terms[...], peer_of(jnp.maximum(b - 1, 0)))
        meta = buf[b, :, BLK * UNIT : UROWS, :].reshape(64, 128)
        lanes = ids((128, LANES), 1) // FR
        wexp = dot_nn(small[...], mark(ids((128, LANES), 0) == lanes + 8 * b))
        right = dot_nn(dot_nt(sel[...], meta).astype(BF16), ind_m[...])
        terms[...] = batch_terms(by_peer, both, seg[...], wexp[:8] + right[:8], wexp[8:])
        return carry

    lax.fori_loop(0, NB, step, 0)
    acc[...] += dot_nn(terms[...], peer_of(NB - 1))

    first = acc[:OWN2]
    grads = v_ref[...] * first + acc[OWN2:] * (1.0 / math.sqrt(D))
    give[...] = grads[OWN:].astype(BF16)
    gcopy = remote(give, got, sib)
    high = grads.astype(BF16)
    hcopy.wait_recv()
    hid_t[...] = hid[...].T
    for j in range(BLK):
        part = dot_nn(hid_t[...], high[:, j * 128 : (j + 1) * 128])
        flat[j * D : (j + 1) * D, :] = part.astype(BF16)
    a = remote(flat.at[rows((1 - core) * HALF, HALF)], rc, sib)
    score = 0.5 * jnp.sum(own_st[:OWN2].astype(F32) * first, axis=0, keepdims=True)
    score = jnp.concatenate(
        [score[:, j * 128 : (j + 1) * 128] for j in range(BLK)]
        + [jnp.zeros((8 - BLK, 128), F32)],
        axis=0,
    )
    tc[core] = score
    b = remote(tc.at[core], tc.at[core], sib)
    gcopy.wait_recv()
    gf_ref[...] = grads[:OWN] + got[...].astype(F32)
    a.wait_recv()
    b.wait_recv()
    sx[...] = (
        flat[rows(core * HALF, HALF), :].astype(F32) + rc[...].astype(F32)
    ).astype(BF16)
    tx[x] = tc[0] + tc[1]

    copies = []
    for s, dev in enumerate(along_x):
        to = (x + s + 1) % 4
        copies.append(remote(sx.at[rows(to * QUARTER, QUARTER)], rx.at[s], dev))
        copies.append(remote(tx.at[x], tx.at[x], dev))
    for c in copies:
        c.wait_recv()
    sy[...] = (
        sx[rows(x * QUARTER, QUARTER), :].astype(F32)
        + rx[0].astype(F32)
        + rx[1].astype(F32)
        + rx[2].astype(F32)
    ).astype(BF16)
    ty[y] = (tx[0] + tx[1]) + (tx[2] + tx[3])

    copies = []
    for s, dev in enumerate(along_y):
        to = (y + s + 1) % 4
        copies.append(remote(sy.at[rows(to * PIECE, PIECE)], ry.at[s], dev))
        copies.append(remote(ty.at[y], ty.at[y], dev))
    for c in copies:
        c.wait_recv()
    rz[z] = (
        sy[rows(y * PIECE, PIECE), :].astype(F32)
        + ry[0].astype(F32)
        + ry[1].astype(F32)
        + ry[2].astype(F32)
    ).astype(BF16)
    tz[z] = (ty[0] + ty[1]) + (ty[2] + ty[3])

    copies = []
    for dev in along_z:
        copies.append(remote(rz.at[z], rz.at[z], dev))
        copies.append(remote(tz.at[z], tz.at[z], dev))
    for c in copies:
        c.wait_recv()
    total = rz[0].astype(F32)
    score = tz[0]
    for i in range(1, 8):
        total = total + rz[i].astype(F32)
        score = score + tz[i]
    score_ref[...] = score
    first = core * HALF + x * QUARTER
    mine = rows(first + y * PIECE, PIECE)
    full[mine, :] = total.astype(BF16)

    copies = [remote(full.at[mine], full.at[mine], dev) for dev in along_y]
    for c in copies:
        c.wait_recv()
    quarter = rows(first, QUARTER)
    copies = [remote(full.at[quarter], full.at[quarter], dev) for dev in along_x]
    for c in copies:
        c.wait_recv()
    half = rows(core * HALF, HALF)
    remote(full.at[half], full.at[half], sib).wait_recv()
    for j in range(BLK):
        out_ref[:, j * 128 : (j + 1) * 128] = full[j * D : (j + 1) * D, :]
    for c in pending:
        c.wait_send()

    def drain(b, carry):
        for s in range(SUB):
            for u in range(4):

                def done():
                    ring(b, u, b, u, sib, s).wait_send()

                if u < 2:
                    done()
                else:
                    pl.when(b < NB - 1)(done)
        return carry

    lax.fori_loop(0, NB, drain, 0)


def local(songs, gain, enc_weight, score_vec, left_local, right_song, clique):
    vmem = pl.BlockSpec(memory_space=pltpu.VMEM)
    gf, weight, total = pl.pallas_call(
        kernel,
        out_shape=(
            jax.ShapeDtypeStruct((OWN, D), F32),
            jax.ShapeDtypeStruct((D, D), BF16),
            jax.ShapeDtypeStruct((8, 128), F32),
        ),
        in_specs=[vmem] * 7,
        out_specs=(vmem,) * 3,
        scratch_shapes=[
            pltpu.VMEM((NB, 4, UROWS, 128), BF16),
            pltpu.VMEM((OWN2, D), BF16),
            pltpu.VMEM((2 * OWN2, D), BF16),
            pltpu.VMEM((D, OWN2), BF16),
            pltpu.VMEM((OWN2, D), BF16),
            pltpu.VMEM((D, OWN2), BF16),
            pltpu.VMEM((2, 16, 256), BF16),
            pltpu.VMEM((LANES, LANES), BF16),
            pltpu.VMEM((64, LANES), BF16),
            pltpu.VMEM((16, 128), BF16),
            pltpu.VMEM((16, 128), BF16),
            pltpu.VMEM((2 * OWN2, LANES), BF16),
            pltpu.VMEM((2 * OWN2, D), F32),
            pltpu.VMEM((OWN, D), BF16),
            pltpu.VMEM((OWN, D), BF16),
            pltpu.VMEM((FLAT, 128), BF16),
            pltpu.VMEM((HALF, 128), BF16),
            pltpu.VMEM((HALF, 128), BF16),
            pltpu.VMEM((3, QUARTER, 128), BF16),
            pltpu.VMEM((QUARTER, 128), BF16),
            pltpu.VMEM((3, PIECE, 128), BF16),
            pltpu.VMEM((8, PIECE, 128), BF16),
            pltpu.VMEM((FLAT, 128), BF16),
            pltpu.VMEM((2, 8, 128), F32),
            pltpu.VMEM((4, 8, 128), F32),
            pltpu.VMEM((4, 8, 128), F32),
            pltpu.VMEM((8, 8, 128), F32),
            pltpu.SemaphoreType.DMA((NB, 4 * SUB)),
            pltpu.SemaphoreType.DMA((NB, 4 * SUB)),
            pltpu.SemaphoreType.DMA((N_COPIES,)),
            pltpu.SemaphoreType.DMA((N_COPIES,)),
        ],
        compiler_params=pltpu.CompilerParams(
            collective_id=0, has_side_effects=True, vmem_limit_bytes=52 * 2**20
        ),
    )(
        songs.reshape(OWN, D),
        gain.reshape(1, D),
        enc_weight,
        score_vec.reshape(1, D),
        left_local.reshape(1, 128),
        right_song.reshape(1, 128),
        clique.reshape(8, 128),
    )
    return (
        gf.reshape(4, FR, D),
        weight.astype(F32),
        total[:BLK].reshape(D),
    )


def solution(mesh):
    in_specs = (
        P(("grp", "dev"), None, None),
        P(),
        P(),
        P(),
        P(("grp", "dev")),
        P(("grp", "dev")),
        P(),
    )
    out_specs = (P(("grp", "dev"), None, None), P(), P())
    return jax.shard_map(local, mesh=mesh, in_specs=in_specs, out_specs=out_specs, check_vma=False)
```

```python
import functools
import math

import jax
import jax.numpy as jnp
from jax import lax
from jax.experimental import pallas as pl
from jax.experimental.pallas import tpu as pltpu
from jax.sharding import PartitionSpec as P

D = 768
FR = 48
OWN = 4 * FR
GRP = 2 * OWN
UNIT = 2 * FR
BLK = D // 128
UROWS = UNIT * BLK + 16
LANES = 8 * FR
NB = 8
STEPS = 2 * NB
POLLS = ((1, 1), (2, 2), (4, 3), (6, 4), (8, 5), (10, 6), (14, 7))
FAR = (0, 0, 1, 3, 1, 3, 2, 2)
PART = (0, 1, 1, 0, 0, 1, 0, 1)
LOSS_SCALE = 16.0
LOG2E = math.log2(math.e)
C0 = 1.0 / (math.sqrt(FR) * math.sqrt(D))
F32 = jnp.float32
BF16 = jnp.bfloat16
MESH = pl.DeviceIdType.MESH


def dot_nn(a, b):
    return jnp.dot(a, b, preferred_element_type=F32)


def dot_nt(a, b):
    return lax.dot_general(a, b, (((1,), (1,)), ((), ())), preferred_element_type=F32)


def dot_tn(a, b):
    return lax.dot_general(a, b, (((0,), (0,)), ((), ())), preferred_element_type=F32)


def col_softmax(scores):
    scale = LOG2E / math.sqrt(D)
    top = jnp.max(scores, axis=0, keepdims=True)
    e = jnp.exp2((scores - top) * scale)
    return e * (1.0 / jnp.sum(e, axis=0, keepdims=True))


def batch_scores(peer, own_t):
    st = dot_nn(peer, own_t)
    scores_x = st[:, :GRP]
    ps, gs = [], []
    for p in range(8):
        prob = col_softmax(scores_x[p * FR : (p + 1) * FR]).astype(BF16)
        pf = prob.astype(F32)
        prod = st[p * FR : (p + 1) * FR, GRP:]
        zz = pf * prod
        ps.append(prob)
        gs.append((zz - pf * jnp.sum(zz, axis=0, keepdims=True)).astype(BF16))
    by_peer = jnp.concatenate(ps, axis=0).T
    grad_peer = jnp.concatenate(gs, axis=0).T
    return by_peer, grad_peer, st.T


def batch_terms(by_peer, grad_peer, both, seg, weights, signs):
    total, first, second, z1s = [], [], [], []
    for a in range(8):
        rows = slice(a * FR, (a + 1) * FR)
        t = both[GRP + a * FR : GRP + (a + 1) * FR]
        p1 = by_peer[rows].astype(F32)
        p2 = col_softmax(both[rows]).astype(BF16).astype(F32)
        z2 = p2 * t
        r2 = jnp.sum(z2, axis=0, keepdims=True)
        total.append(jnp.sum(p1 * t, axis=0, keepdims=True) + r2)
        first.append(p1 + p2)
        second.append(z2 - p2 * r2 + grad_peer[rows].astype(F32))
    sums = jnp.concatenate(total, axis=0)
    high = sums.astype(BF16)
    low = (sums - high.astype(F32)).astype(BF16)
    spread = dot_nn(jnp.concatenate([high, low], axis=0), seg)
    logit = (spread[:8] + spread[8:]) * C0
    coef = weights * signs * (-LOSS_SCALE * C0) / (1.0 + jnp.exp(signs * logit))
    out1, out2 = [], []
    for a in range(8):
        c = coef[a : a + 1]
        out1.append((c * first[a]).astype(BF16))
        out2.append((c * second[a]).astype(BF16))
    return jnp.concatenate(out1 + out2, axis=0)


CHUNKS = 2
PIECE = 80
CORE = 16 * PIECE
CHUNK = 2 * CORE
FLAT = CHUNKS * CHUNK
WEIGHT = BLK * D
N_COPIES = 3 + 6 + CHUNKS * (1 + 15 + 7 + 15 + 1)


def kernel(
    x_hbm, gain_hbm, w_hbm, v_hbm, left_hbm, right_hbm, clique_hbm,
    gf_ref, out_ref, score_ref,
    x_ref, gain_ref, w_ref, v_ref, left_ref, right_ref, clique_ref, in_sems,
    xin, buf, own_st, own_t, hid, hid_t, cnt, seg, ind_m, sel, small, terms, acc,
    give, back,
    flat, rc, half, rp, rz, full,
    csend, crecv, xsend, xrecv, sems, rems,
):
    y = lax.axis_index("grp")
    me = lax.axis_index("dev")
    core = me % 2
    chip = me // 2
    x = chip % 4
    z = chip // 4
    sib = (y, me + 1 - 2 * core)
    along_x = [(y, (z * 4 + (x + s) % 4) * 2 + core) for s in range(1, 4)]
    along_z = [(y, (((z + s) % 8) * 4 + x) * 2 + core) for s in range(1, 8)]
    spread = [(sy, sx) for sy in range(4) for sx in range(4) if sy or sx]
    plane = [((y + sy) % 4, (z * 4 + (x + sx) % 4) * 2 + core) for sy, sx in spread]
    x_up, x_far, x_down = along_x
    z_up, z_down = along_z[0], along_z[6]

    inputs = [
        pltpu.make_async_copy(src, dst, in_sems.at[n])
        for n, (src, dst) in enumerate(
            (
                (x_hbm, x_ref),
                (left_hbm, left_ref),
                (right_hbm, right_ref),
                (w_hbm, w_ref),
                (gain_hbm, gain_ref),
                (v_hbm, v_ref),
                (clique_hbm, clique_ref),
            )
        )
    ]
    for copy in inputs:
        copy.start()
    barrier = pltpu.get_barrier_semaphore()
    for dev in [sib] + plane + along_z:
        pl.semaphore_signal(barrier, inc=1, device_id=dev, device_id_type=MESH)

    def column(sb, su, db, du, dev):
        return pltpu.make_async_remote_copy(
            src_ref=buf.at[sb, su], dst_ref=buf.at[db, du],
            send_sem=csend.at[db, du], recv_sem=crecv.at[db, du],
            device_id=dev, device_id_type=MESH,
        )

    def row_unit(src, dst, dev):
        return pltpu.make_async_remote_copy(
            src_ref=xin.at[src], dst_ref=xin.at[dst],
            send_sem=xsend.at[dst], recv_sem=xrecv.at[dst],
            device_id=dev, device_id_type=MESH,
        )

    count = [0]
    pending = []

    def remote(src, dst, dev):
        i = count[0]
        count[0] += 1
        copy = pltpu.make_async_remote_copy(
            src_ref=src, dst_ref=dst, send_sem=sems.at[i], recv_sem=rems.at[i],
            device_id=dev, device_id_type=MESH,
        )
        copy.start()
        pending.append(copy)
        return copy

    def rows(start, size):
        return pl.ds(pl.multiple_of(start, 16), size)

    def ids(shape, dim):
        return lax.broadcasted_iota(jnp.int32, shape, dim)

    def mark(cond):
        return jnp.where(cond, 1.0, 0.0).astype(BF16)

    for copy in inputs[:3]:
        copy.wait()
    for k in range(2):
        xin[k] = x_ref[k * UNIT : (k + 1) * UNIT]
    hot_left = mark(ids((16, 128), 0) == left_ref[...])
    hot_right = mark(ids((256, 128), 0) == right_ref[...] - y * 256)
    counts = dot_nt(hot_left, hot_right)
    cnt[0] = counts.astype(BF16)
    pl.semaphore_wait(barrier, 23)
    row_unit(1, 2, x_down).start()
    row_unit(0, 3, x_up).start()
    row_unit(0, 4, x_down).start()
    row_unit(1, 5, x_up).start()
    tables = [remote(cnt.at[0], cnt.at[3 - s], dev) for s, dev in enumerate(along_x)]

    for copy in inputs[3:]:
        copy.wait()

    def wide(ref):
        return jnp.concatenate([ref[j : j + 1, :] for j in range(BLK)], axis=1)

    gain = wide(gain_ref)
    score_vec = wide(v_ref)

    def encode(songs):
        values = songs.astype(F32)
        square_mean = jnp.mean(values * values, axis=-1, keepdims=True)
        hidden = (values * lax.rsqrt(square_mean + 1e-06) * gain).astype(BF16)
        feats = (values + dot_nn(hidden, w_ref[...])).astype(BF16)
        return hidden, feats

    hidden, feats = encode(x_ref[...])
    hid[:OWN] = hidden
    own_st[0, :OWN] = feats
    for k in range(2):
        for j in range(BLK):
            buf[0, k, j * UNIT : (j + 1) * UNIT, :] = feats[
                k * UNIT : (k + 1) * UNIT, j * 128 : (j + 1) * 128
            ]
        lines = [
            counts[2 * k + l : 2 * k + l + 1, h * 128 : (h + 1) * 128]
            for l in range(2)
            for h in range(2)
        ]
        buf[0, k, BLK * UNIT : UROWS, :] = jnp.concatenate(
            lines + [jnp.zeros((12, 128), F32)], axis=0
        ).astype(BF16)
    for k in range(2):
        column(0, k, 1 + k, 0, z_up).start()
        column(0, k, 1 + k, 1, z_down).start()
        column(0, k, 0, 2 + k, sib).start()

    shape = (LANES, LANES)
    seg[...] = mark(ids(shape, 0) // FR == ids(shape, 1) // FR)
    shape = (64, LANES)
    row = ids(shape, 0)
    song = 2 * (row // 16) + (row % 16) // 2
    right_row = jnp.logical_and(row % 16 < 4, row % 2 == z // 4)
    ind_m[...] = mark(jnp.logical_and(right_row, song == ids(shape, 1) // FR))
    acc[...] = jnp.zeros_like(acc)
    terms[...] = jnp.zeros_like(terms)

    lane = ids((1, 128), 1)
    b = lane // 8
    u = (lane % 8) // 2
    way = u % 2
    t = (b + 1) // 2
    dz = jnp.where(b == 0, 0, jnp.where(way == 0, 8 - t % 8, t))
    k = jnp.where(jnp.logical_or(b == 0, b == NB - 1), way, (b + 1) % 2)
    held = (((z + dz) % 8) * 4 + x) * 2 + jnp.where(u < 2, core, 1 - core)
    landing = held * 4 + 2 * k + lane % 2
    hot = mark(ids((256, 128), 0) == landing)
    group_rows = [clique_ref[pl.ds(2 * y + h, 1), :] for h in range(2)]
    theirs = jnp.concatenate(group_rows, axis=1).astype(F32)
    near_row = clique_ref[pl.ds(2 * y + z // 4, 1), :].astype(F32)
    for copy in tables:
        copy.wait_recv()
    for r in range(2):
        shape = (16, 128)
        row = ids(shape, 0)
        number = row * 0 - 1
        for w in range(4):
            first = ((z % 4) * 4 + (x + FAR[4 * r + w]) % 4) * 8 + core * 4 + 2 * PART[4 * r + w]
            number = jnp.where(row // 2 == w, first + row % 2, number)
        chosen = ids(shape, 1) == number
        sel[r] = mark(chosen)
        mine = jnp.sum(jnp.where(chosen, near_row, 0.0), axis=1, keepdims=True)[:8]
        signs = jnp.where(mine == theirs, 1.0, -1.0)
        left = [
            cnt[FAR[4 * r + w]].astype(F32)[2 * PART[4 * r + w] : 2 * PART[4 * r + w] + 2]
            for w in range(4)
        ]
        table = jnp.concatenate(left + [signs], axis=0).astype(BF16)
        small[r] = dot_nn(table, hot).astype(BF16)

    def prepare(r):
        feats = own_st[r, :GRP]
        own_st[r, GRP:] = (feats.astype(F32) * score_vec).astype(BF16)
        own_t[r] = own_st[r].T

    def arrived(b, u):
        column(b, u, b, u, sib).wait_recv()

    for u in (2, 3):
        row_unit(u, u, x_up).wait_recv()
    row_unit(3, 6, x_up).start()
    row_unit(2, 7, x_down).start()
    hidden, feats = encode(xin[2:4].reshape(OWN, D))
    hid[OWN:GRP] = hidden
    own_st[0, OWN:GRP] = feats
    prepare(0)

    def peer_of(b):
        return jnp.concatenate(
            [
                buf[b, :, j * UNIT : (j + 1) * UNIT, :].reshape(LANES, 128)
                for j in range(BLK)
            ],
            axis=1,
        )

    def order(i):
        late = (i + 10) // 16
        return (
            (1 - late) * (i % 3) + late * (i // 2),
            (1 - late) * (i // 3) + late * ((i + i // 14) % 2),
        )

    def step(i, carry):
        b, r = order(i)

        for at, ahead in POLLS:

            @pl.when(i == at)
            def _():
                for way, dev in ((0, z_up), (1, z_down)):
                    arrived(ahead, way)
                    if ahead < 5:
                        column(ahead, way, ahead + 2, way, dev).start()
                    elif ahead == 5 + way:
                        column(ahead, way, 7, way, dev).start()
                    column(ahead, way, ahead, 2 + way, sib).start()

        @pl.when(i == 3)
        def _():
            for u in (4, 5, 6, 7):
                row_unit(u, u, x_up).wait_recv()
            hidden, feats = encode(xin[4:8].reshape(GRP, D))
            hid[GRP:] = hidden
            own_st[1, :GRP] = feats
            prepare(1)
            hid_t[...] = hid[...].T

        @pl.when(jnp.logical_or(i < 3, jnp.logical_and(i >= 6, i % 2 == 0)))
        def _():
            for k in range(2):
                arrived(b, 2 + k)

        peer = peer_of(b)
        by_peer, grad_peer, both = batch_scores(peer, own_t[r])

        before, rows_before = order(jnp.maximum(i - 1, 0))
        acc[rows_before] += dot_nn(terms[...], peer_of(before))
        meta = buf[b, :, BLK * UNIT : UROWS, :].reshape(64, 128)
        lanes = ids((128, LANES), 1) // FR
        wexp = dot_nn(small[r], mark(ids((128, LANES), 0) == lanes + 8 * b))
        right = dot_nn(dot_nt(sel[r], meta).astype(BF16), ind_m[...])
        terms[...] = batch_terms(
            by_peer, grad_peer, both, seg[...], wexp[:8] + right[:8], wexp[8:]
        )
        return carry

    lax.fori_loop(0, STEPS, step, 0)
    acc[0] += dot_nn(terms[...], peer_of(NB - 1))

    score = jnp.zeros((1, D), F32)
    for r in range(2):
        first = acc[r, :GRP]
        grads = score_vec * first + acc[r, GRP:] * (1.0 / math.sqrt(D))
        if r == 0:
            gf_ref[...] = grads[:OWN]
        give[4 * r : 4 * r + 4] = grads.astype(BF16).reshape(4, UNIT, D)
        score += 0.5 * jnp.sum(own_st[r, :GRP].astype(F32) * first, axis=0, keepdims=True)
    for j in range(BLK):
        high = give[:, :, j * 128 : (j + 1) * 128].reshape(2 * GRP, 128)
        flat[j * D : (j + 1) * D, :] = dot_nn(hid_t[...], high).astype(BF16)
    flat[WEIGHT : WEIGHT + 16, :] = jnp.concatenate(
        [score[:, j * 128 : (j + 1) * 128] for j in range(BLK)]
        + [jnp.zeros((16 - BLK, 128), F32)],
        axis=0,
    ).astype(BF16)
    flat[WEIGHT + 16 :, :] = jnp.zeros((FLAT - WEIGHT - 16, 128), BF16)

    chunks = range(CHUNKS)
    copies = [
        remote(flat.at[rows(h * CHUNK + (1 - core) * CORE, CORE)], rc.at[h], sib)
        for h in chunks
    ]
    plane_copies = []
    for h in chunks:
        copies[h].wait_recv()
        half[h] = (
            flat[rows(h * CHUNK + core * CORE, CORE), :].astype(F32) + rc[h].astype(F32)
        ).astype(BF16)
        plane_copies.append(
            [
                remote(
                    half.at[h, rows((((y + sy) % 4) * 4 + (x + sx) % 4) * PIECE, PIECE)],
                    rp.at[h, n],
                    plane[n],
                )
                for n, (sy, sx) in enumerate(spread)
            ]
        )
    returned = []
    for k in range(2):
        returned.append(remote(give.at[(4, 2)[k]], back.at[k], x_up))
        returned.append(remote(give.at[(3, 5)[k]], back.at[2 + k], x_down))
    for k in range(2):
        returned.append(remote(give.at[6 + k], back.at[4 + k], x_far))
    line_copies = []
    for h in chunks:
        for c in plane_copies[h]:
            c.wait_recv()
        total = half[h, rows((y * 4 + x) * PIECE, PIECE), :].astype(F32)
        for n in range(15):
            total = total + rp[h, n].astype(F32)
        rz[h, z] = total.astype(BF16)
        line_copies.append([remote(rz.at[h, z], rz.at[h, z], dev) for dev in along_z])
    plane_copies = []
    for h in chunks:
        for c in line_copies[h]:
            c.wait_recv()
        total = rz[h, 0].astype(F32)
        for n in range(1, 8):
            total = total + rz[h, n].astype(F32)
        mine = rows(h * CHUNK + core * CORE + (y * 4 + x) * PIECE, PIECE)
        full[mine, :] = total.astype(BF16)
        plane_copies.append([remote(full.at[mine], full.at[mine], dev) for dev in plane])
    copies = []
    for h in chunks:
        for c in plane_copies[h]:
            c.wait_recv()
        same = rows(h * CHUNK + core * CORE, CORE)
        copies.append(remote(full.at[same], full.at[same], sib))
    for copy in returned:
        copy.wait_recv()
    for k in range(2):
        part = slice(k * UNIT, (k + 1) * UNIT)
        gf_ref[part, :] = (
            (gf_ref[part, :] + back[k].astype(F32))
            + (back[2 + k].astype(F32) + back[4 + k].astype(F32))
        )
    for c in copies:
        c.wait_recv()
    for j in range(BLK):
        out_ref[:, j * 128 : (j + 1) * 128] = full[j * D : (j + 1) * D, :]
    score_ref[...] = full[WEIGHT : WEIGHT + 16, :].astype(F32)[:8]
    for c in pending:
        c.wait_send()
    for u in range(2, 8):
        row_unit(u, u, x_up).wait_send()
    for b in range(NB):
        for u in range(4):
            if b or u > 1:
                column(b, u, b, u, sib).wait_send()


def local(songs, gain, enc_weight, score_vec, left_local, right_song, clique):
    vmem = pl.BlockSpec(memory_space=pltpu.VMEM)
    gf, weight, total = pl.pallas_call(
        kernel,
        out_shape=(
            jax.ShapeDtypeStruct((OWN, D), F32),
            jax.ShapeDtypeStruct((D, D), BF16),
            jax.ShapeDtypeStruct((8, 128), F32),
        ),
        in_specs=[pl.BlockSpec(memory_space=pl.ANY)] * 7,
        out_specs=(vmem,) * 3,
        scratch_shapes=[
            pltpu.VMEM((OWN, D), BF16),
            pltpu.VMEM((BLK, 128), F32),
            pltpu.VMEM((D, D), BF16),
            pltpu.VMEM((BLK, 128), F32),
            pltpu.VMEM((1, 128), jnp.int32),
            pltpu.VMEM((1, 128), jnp.int32),
            pltpu.VMEM((8, 128), jnp.int32),
            pltpu.SemaphoreType.DMA((7,)),
            pltpu.VMEM((8, UNIT, D), BF16),
            pltpu.VMEM((NB, 4, UROWS, 128), BF16),
            pltpu.VMEM((2, 2 * GRP, D), BF16),
            pltpu.VMEM((2, D, 2 * GRP), BF16),
            pltpu.VMEM((2 * GRP, D), BF16),
            pltpu.VMEM((D, 2 * GRP), BF16),
            pltpu.VMEM((4, 16, 256), BF16),
            pltpu.VMEM((LANES, LANES), BF16),
            pltpu.VMEM((64, LANES), BF16),
            pltpu.VMEM((2, 16, 128), BF16),
            pltpu.VMEM((2, 16, 128), BF16),
            pltpu.VMEM((2 * GRP, LANES), BF16),
            pltpu.VMEM((2, 2 * GRP, D), F32),
            pltpu.VMEM((8, UNIT, D), BF16),
            pltpu.VMEM((6, UNIT, D), BF16),
            pltpu.VMEM((FLAT, 128), BF16),
            pltpu.VMEM((CHUNKS, CORE, 128), BF16),
            pltpu.VMEM((CHUNKS, CORE, 128), BF16),
            pltpu.VMEM((CHUNKS, 15, PIECE, 128), BF16),
            pltpu.VMEM((CHUNKS, 8, PIECE, 128), BF16),
            pltpu.VMEM((FLAT, 128), BF16),
            pltpu.SemaphoreType.DMA((NB, 4)),
            pltpu.SemaphoreType.DMA((NB, 4)),
            pltpu.SemaphoreType.DMA((8,)),
            pltpu.SemaphoreType.DMA((8,)),
            pltpu.SemaphoreType.DMA((N_COPIES,)),
            pltpu.SemaphoreType.DMA((N_COPIES,)),
        ],
        compiler_params=pltpu.CompilerParams(
            collective_id=0, has_side_effects=True, vmem_limit_bytes=60 * 2**20
        ),
    )(
        songs.reshape(OWN, D),
        gain.reshape(BLK, 128),
        enc_weight,
        score_vec.reshape(BLK, 128),
        left_local.reshape(1, 128),
        right_song.reshape(1, 128),
        clique.reshape(8, 128),
    )
    return (
        gf.reshape(4, FR, D),
        weight.astype(F32),
        total[:BLK].reshape(D),
    )


def solution(mesh):
    in_specs = (
        P(("grp", "dev"), None, None),
        P(),
        P(),
        P(),
        P(("grp", "dev")),
        P(("grp", "dev")),
        P(),
    )
    out_specs = (P(("grp", "dev"), None, None), P(), P())
    return jax.shard_map(local, mesh=mesh, in_specs=in_specs, out_specs=out_specs, check_vma=False)
```

```python
import functools
import math

import jax
import jax.numpy as jnp
from jax import lax
from jax.experimental import pallas as pl
from jax.experimental.pallas import tpu as pltpu
from jax.sharding import PartitionSpec as P

D = 768
FR = 48
OWN = 4 * FR
GRP = 2 * OWN
UNIT = 2 * FR
BLK = D // 128
UROWS = UNIT * BLK + 16
LANES = 8 * FR
NB = 8
STEPS = 2 * NB
POLLS = ((0, 1), (1, 2), (3, 3), (4, 4), (6, 5), (8, 6), (12, 7))
FAR = (0, 0, 1, 3, 1, 3, 2, 2)
PART = (0, 1, 1, 0, 0, 1, 0, 1)
LOSS_SCALE = 16.0
LOG2E = math.log2(math.e)
C0 = 1.0 / (math.sqrt(FR) * math.sqrt(D))
F32 = jnp.float32
BF16 = jnp.bfloat16
MESH = pl.DeviceIdType.MESH


def dot_nn(a, b):
    return jnp.dot(a, b, preferred_element_type=F32)


def dot_nt(a, b):
    return lax.dot_general(a, b, (((1,), (1,)), ((), ())), preferred_element_type=F32)


def dot_tn(a, b):
    return lax.dot_general(a, b, (((0,), (0,)), ((), ())), preferred_element_type=F32)


def col_softmax(scores):
    scale = LOG2E / math.sqrt(D)
    top = jnp.max(scores, axis=0, keepdims=True)
    e = jnp.exp2((scores - top) * scale)
    return e * (1.0 / jnp.sum(e, axis=0, keepdims=True))


def batch_scores(peer, own_t):
    st = dot_nn(peer, own_t)
    scores_x = st[:, :GRP]
    ps, gs = [], []
    for p in range(8):
        prob = col_softmax(scores_x[p * FR : (p + 1) * FR]).astype(BF16)
        pf = prob.astype(F32)
        prod = st[p * FR : (p + 1) * FR, GRP:]
        zz = pf * prod
        ps.append(prob)
        gs.append((zz - pf * jnp.sum(zz, axis=0, keepdims=True)).astype(BF16))
    by_peer = jnp.concatenate(ps, axis=0).T
    grad_peer = jnp.concatenate(gs, axis=0).T
    return by_peer, grad_peer, st.T


def batch_terms(by_peer, grad_peer, both, seg, weights, signs):
    total, first, second, z1s = [], [], [], []
    for a in range(8):
        rows = slice(a * FR, (a + 1) * FR)
        t = both[GRP + a * FR : GRP + (a + 1) * FR]
        p1 = by_peer[rows].astype(F32)
        p2 = col_softmax(both[rows]).astype(BF16).astype(F32)
        z2 = p2 * t
        r2 = jnp.sum(z2, axis=0, keepdims=True)
        total.append(jnp.sum(p1 * t, axis=0, keepdims=True) + r2)
        first.append(p1 + p2)
        second.append(z2 - p2 * r2 + grad_peer[rows].astype(F32))
    sums = jnp.concatenate(total, axis=0)
    high = sums.astype(BF16)
    low = (sums - high.astype(F32)).astype(BF16)
    spread = dot_nn(jnp.concatenate([high, low], axis=0), seg)
    logit = (spread[:8] + spread[8:]) * C0
    coef = weights * signs * (-LOSS_SCALE * C0) / (1.0 + jnp.exp(signs * logit))
    out1, out2 = [], []
    for a in range(8):
        c = coef[a : a + 1]
        out1.append((c * first[a]).astype(BF16))
        out2.append((c * second[a]).astype(BF16))
    return jnp.concatenate(out1 + out2, axis=0)


CHUNKS = 2
PIECE = 80
CORE = 16 * PIECE
CHUNK = 2 * CORE
FLAT = CHUNKS * CHUNK
WEIGHT = BLK * D
N_COPIES = 3 + 6 + CHUNKS * (1 + 15 + 7 + 15 + 1)


def kernel(
    x_hbm, gain_hbm, w_hbm, v_hbm, left_hbm, right_hbm, clique_hbm,
    gf_ref, out_ref, score_ref,
    x_ref, gain_ref, w_ref, v_ref, left_ref, right_ref, clique_ref, in_sems,
    xin, buf, own_st, own_t, hid, hid_t, cnt, seg, ind_m, sel, small, terms, acc,
    give, back,
    flat, rc, half, rp, rz, full,
    csend, crecv, xsend, xrecv, sems, rems,
):
    y = lax.axis_index("grp")
    me = lax.axis_index("dev")
    core = me % 2
    chip = me // 2
    x = chip % 4
    z = chip // 4
    sib = (y, me + 1 - 2 * core)
    along_x = [(y, (z * 4 + (x + s) % 4) * 2 + core) for s in range(1, 4)]
    along_z = [(y, (((z + s) % 8) * 4 + x) * 2 + core) for s in range(1, 8)]
    spread = [(sy, sx) for sy in range(4) for sx in range(4) if sy or sx]
    plane = [((y + sy) % 4, (z * 4 + (x + sx) % 4) * 2 + core) for sy, sx in spread]
    x_up, x_far, x_down = along_x
    z_up, z_down = along_z[0], along_z[6]

    inputs = [
        pltpu.make_async_copy(src, dst, in_sems.at[n])
        for n, (src, dst) in enumerate(
            (
                (x_hbm, x_ref),
                (left_hbm, left_ref),
                (right_hbm, right_ref),
                (w_hbm, w_ref),
                (gain_hbm, gain_ref),
                (v_hbm, v_ref),
                (clique_hbm, clique_ref),
            )
        )
    ]
    for copy in inputs:
        copy.start()
    barrier = pltpu.get_barrier_semaphore()
    for dev in [sib] + plane + along_z:
        pl.semaphore_signal(barrier, inc=1, device_id=dev, device_id_type=MESH)

    def column(sb, su, db, du, dev):
        return pltpu.make_async_remote_copy(
            src_ref=buf.at[sb, su], dst_ref=buf.at[db, du],
            send_sem=csend.at[db, du], recv_sem=crecv.at[db, du],
            device_id=dev, device_id_type=MESH,
        )

    def row_unit(src, dst, dev):
        source = xin.at[src] if src > 1 else x_hbm.at[pl.ds(src * UNIT, UNIT)]
        return pltpu.make_async_remote_copy(
            src_ref=source, dst_ref=xin.at[dst],
            send_sem=xsend.at[dst], recv_sem=xrecv.at[dst],
            device_id=dev, device_id_type=MESH,
        )

    count = [0]
    pending = []

    def remote(src, dst, dev):
        i = count[0]
        count[0] += 1
        copy = pltpu.make_async_remote_copy(
            src_ref=src, dst_ref=dst, send_sem=sems.at[i], recv_sem=rems.at[i],
            device_id=dev, device_id_type=MESH,
        )
        copy.start()
        pending.append(copy)
        return copy

    def rows(start, size):
        return pl.ds(pl.multiple_of(start, 16), size)

    def ids(shape, dim):
        return lax.broadcasted_iota(jnp.int32, shape, dim)

    def mark(cond):
        return jnp.where(cond, 1.0, 0.0).astype(BF16)

    pl.semaphore_wait(barrier, 23)
    row_unit(1, 2, x_down).start()
    row_unit(0, 3, x_up).start()
    row_unit(0, 4, x_down).start()
    row_unit(1, 5, x_up).start()
    for copy in inputs[1:3]:
        copy.wait()
    hot_left = mark(ids((16, 128), 0) == left_ref[...])
    hot_right = mark(ids((256, 128), 0) == right_ref[...] - y * 256)
    counts = dot_nt(hot_left, hot_right)
    cnt[0] = counts.astype(BF16)
    tables = [remote(cnt.at[0], cnt.at[3 - s], dev) for s, dev in enumerate(along_x)]

    for copy in inputs[:1] + inputs[3:]:
        copy.wait()

    def wide(ref):
        return jnp.concatenate([ref[j : j + 1, :] for j in range(BLK)], axis=1)

    gain = wide(gain_ref)
    score_vec = wide(v_ref)

    def encode(songs):
        values = songs.astype(F32)
        square_mean = jnp.mean(values * values, axis=-1, keepdims=True)
        hidden = (values * lax.rsqrt(square_mean + 1e-06) * gain).astype(BF16)
        feats = (values + dot_nn(hidden, w_ref[...])).astype(BF16)
        return hidden, feats

    hidden, feats = encode(x_ref[...])
    hid[:OWN] = hidden
    for k in range(2):
        for j in range(BLK):
            buf[0, k, j * UNIT : (j + 1) * UNIT, :] = feats[
                k * UNIT : (k + 1) * UNIT, j * 128 : (j + 1) * 128
            ]
        lines = [
            counts[2 * k + l : 2 * k + l + 1, h * 128 : (h + 1) * 128]
            for l in range(2)
            for h in range(2)
        ]
        buf[0, k, BLK * UNIT : UROWS, :] = jnp.concatenate(
            lines + [jnp.zeros((12, 128), F32)], axis=0
        ).astype(BF16)
    for k in range(2):
        column(0, k, 1 + k, 0, z_up).start()
        column(0, k, 1 + k, 1, z_down).start()
        column(0, k, 0, 2 + k, sib).start()

    lane_song = ids((1, LANES), 1) // FR
    for a in range(8):
        seg[a * FR : (a + 1) * FR] = mark(ids((FR, LANES), 0) * 0 + lane_song == a)
    row = ids((64, 1), 0)
    song = 2 * (row // 16) + (row % 16) // 2
    song = jnp.where(jnp.logical_and(row % 16 < 4, row % 2 == z // 4), song, -1)
    ind_m[...] = mark(song == lane_song)
    acc[...] = jnp.zeros_like(acc)
    terms[...] = jnp.zeros_like(terms)

    lane = ids((1, 128), 1)
    b = lane // 8
    u = (lane % 8) // 2
    way = u % 2
    t = (b + 1) // 2
    dz = jnp.where(b == 0, 0, jnp.where(way == 0, 8 - t % 8, t))
    k = jnp.where(jnp.logical_or(b == 0, b == NB - 1), way, (b + 1) % 2)
    held = (((z + dz) % 8) * 4 + x) * 2 + jnp.where(u < 2, core, 1 - core)
    landing = held * 4 + 2 * k + lane % 2
    hot = mark(ids((256, 128), 0) == landing)
    group_rows = [clique_ref[pl.ds(2 * y + h, 1), :] for h in range(2)]
    theirs = jnp.concatenate(group_rows, axis=1).astype(F32)
    near_row = clique_ref[pl.ds(2 * y + z // 4, 1), :].astype(F32)
    for copy in tables:
        copy.wait_recv()
    for r in range(2):
        shape = (16, 128)
        row = ids(shape, 0)
        number = row * 0 - 1
        for w in range(4):
            first = ((z % 4) * 4 + (x + FAR[4 * r + w]) % 4) * 8 + core * 4 + 2 * PART[4 * r + w]
            number = jnp.where(row // 2 == w, first + row % 2, number)
        chosen = ids(shape, 1) == number
        sel[r] = mark(chosen)
        mine = jnp.sum(jnp.where(chosen, near_row, 0.0), axis=1, keepdims=True)[:8]
        signs = jnp.where(mine == theirs, 1.0, -1.0)
        left = [
            cnt[FAR[4 * r + w]].astype(F32)[2 * PART[4 * r + w] : 2 * PART[4 * r + w] + 2]
            for w in range(4)
        ]
        table = jnp.concatenate(left + [signs], axis=0).astype(BF16)
        small[r] = dot_nn(table, hot).astype(BF16)

    def prepare(r, start, feats):
        size = feats.shape[0]
        scaled = (feats.astype(F32) * score_vec).astype(BF16)
        own_st[r, start : start + size] = feats
        own_t[r, :, start : start + size] = feats.T
        own_t[r, :, GRP + start : GRP + start + size] = scaled.T

    def arrived(b, u):
        column(b, u, b, u, sib).wait_recv()

    prepare(0, 0, feats)
    for u in (2, 3):
        row_unit(u, u, x_up).wait_recv()
    row_unit(3, 6, x_up).start()
    row_unit(2, 7, x_down).start()
    hidden, feats = encode(xin[2:4].reshape(OWN, D))
    hid[OWN:GRP] = hidden
    prepare(0, OWN, feats)

    def peer_of(b):
        return jnp.concatenate(
            [
                buf[b, :, j * UNIT : (j + 1) * UNIT, :].reshape(LANES, 128)
                for j in range(BLK)
            ],
            axis=1,
        )

    def order(i):
        late = (i + 10) // 16
        return (
            (1 - late) * (i % 3) + late * (i // 2),
            (1 - late) * (i // 3) + late * ((i + i // 14) % 2),
        )

    def step(i, carry):
        b, r = order(i)

        for at, ahead in POLLS:

            @pl.when(i == at)
            def _():
                for way, dev in ((0, z_up), (1, z_down)):
                    arrived(ahead, way)
                    if ahead < 5:
                        column(ahead, way, ahead + 2, way, dev).start()
                    elif ahead == 5 + way:
                        column(ahead, way, 7, way, dev).start()
                    column(ahead, way, ahead, 2 + way, sib).start()

        @pl.when(i == 3)
        def _():
            for u in (4, 5, 6, 7):
                row_unit(u, u, x_up).wait_recv()
            hidden, feats = encode(xin[4:8].reshape(GRP, D))
            hid[GRP:] = hidden
            prepare(1, 0, feats)
            hid_t[...] = hid[...].T

        @pl.when(jnp.logical_or(i < 3, jnp.logical_and(i >= 6, i % 2 == 0)))
        def _():
            for k in range(2):
                arrived(b, 2 + k)

        peer = peer_of(b)
        by_peer, grad_peer, both = batch_scores(peer, own_t[r])

        before, rows_before = order(jnp.maximum(i - 1, 0))
        acc[rows_before] += dot_nn(terms[...], peer_of(before))
        meta = buf[b, :, BLK * UNIT : UROWS, :].reshape(64, 128)
        wexp = dot_nn(small[r], mark(ids((128, LANES), 0) == lane_song + 8 * b))
        right = dot_nn(dot_nt(sel[r], meta).astype(BF16), ind_m[...])
        terms[...] = batch_terms(
            by_peer, grad_peer, both, seg[...], wexp[:8] + right[:8], wexp[8:]
        )
        return carry

    lax.fori_loop(0, STEPS, step, 0)
    score = jnp.zeros((1, D), F32)
    returned = []

    def give_back(part, slot, dev):
        returned.append(remote(give.at[part], back.at[slot], dev))

    for r in (1, 0):
        if r == 0:
            acc[0] += dot_nn(terms[...], peer_of(NB - 1))
        first = acc[r, :GRP]
        grads = score_vec * first + acc[r, GRP:] * (1.0 / math.sqrt(D))
        if r == 0:
            gf_ref[...] = grads[:OWN]
        give[4 * r : 4 * r + 4] = grads.astype(BF16).reshape(4, UNIT, D)
        if r == 1:
            give_back(6, 4, x_far)
            give_back(7, 5, x_far)
            give_back(4, 0, x_up)
            give_back(5, 3, x_down)
        score += 0.5 * jnp.sum(own_st[r].astype(F32) * first, axis=0, keepdims=True)
    for j in range(BLK):
        high = give[:, :, j * 128 : (j + 1) * 128].reshape(2 * GRP, 128)
        flat[j * D : (j + 1) * D, :] = dot_nn(hid_t[...], high).astype(BF16)
    flat[WEIGHT : WEIGHT + 16, :] = jnp.concatenate(
        [score[:, j * 128 : (j + 1) * 128] for j in range(BLK)]
        + [jnp.zeros((16 - BLK, 128), F32)],
        axis=0,
    ).astype(BF16)
    flat[WEIGHT + 16 :, :] = jnp.zeros((FLAT - WEIGHT - 16, 128), BF16)

    chunks = range(CHUNKS)
    copies = [
        remote(flat.at[rows(h * CHUNK + (1 - core) * CORE, CORE)], rc.at[h], sib)
        for h in chunks
    ]
    plane_copies = []
    for h in chunks:
        copies[h].wait_recv()
        half[h] = (
            flat[rows(h * CHUNK + core * CORE, CORE), :].astype(F32) + rc[h].astype(F32)
        ).astype(BF16)
        plane_copies.append(
            [
                remote(
                    half.at[h, rows((((y + sy) % 4) * 4 + (x + sx) % 4) * PIECE, PIECE)],
                    rp.at[h, n],
                    plane[n],
                )
                for n, (sy, sx) in enumerate(spread)
            ]
        )
    give_back(2, 1, x_up)
    give_back(3, 2, x_down)
    line_copies = []
    for h in chunks:
        for c in plane_copies[h]:
            c.wait_recv()
        total = half[h, rows((y * 4 + x) * PIECE, PIECE), :].astype(F32)
        for n in range(15):
            total = total + rp[h, n].astype(F32)
        rz[h, z] = total.astype(BF16)
        line_copies.append([remote(rz.at[h, z], rz.at[h, z], dev) for dev in along_z])
    plane_copies = []
    for h in chunks:
        for c in line_copies[h]:
            c.wait_recv()
        total = rz[h, 0].astype(F32)
        for n in range(1, 8):
            total = total + rz[h, n].astype(F32)
        mine = rows(h * CHUNK + core * CORE + (y * 4 + x) * PIECE, PIECE)
        full[mine, :] = total.astype(BF16)
        plane_copies.append([remote(full.at[mine], full.at[mine], dev) for dev in plane])
    copies = []
    for h in chunks:
        for c in plane_copies[h]:
            c.wait_recv()
        same = rows(h * CHUNK + core * CORE, CORE)
        copies.append(remote(full.at[same], full.at[same], sib))
    for copy in returned:
        copy.wait_recv()
    for k in range(2):
        part = slice(k * UNIT, (k + 1) * UNIT)
        gf_ref[part, :] = (
            (gf_ref[part, :] + back[k].astype(F32))
            + (back[2 + k].astype(F32) + back[4 + k].astype(F32))
        )
    for c in copies:
        c.wait_recv()
    for j in range(BLK):
        out_ref[:, j * 128 : (j + 1) * 128] = full[j * D : (j + 1) * D, :]
    score_ref[...] = full[WEIGHT : WEIGHT + 16, :].astype(F32)[:BLK]
    for c in pending:
        c.wait_send()
    for u in range(2, 8):
        row_unit(u, u, x_up).wait_send()
    for b in range(NB):
        for u in range(4):
            if b or u > 1:
                column(b, u, b, u, sib).wait_send()


def local(songs, gain, enc_weight, score_vec, left_local, right_song, clique):
    vmem = pl.BlockSpec(memory_space=pltpu.VMEM)
    gf, weight, total = pl.pallas_call(
        kernel,
        out_shape=(
            jax.ShapeDtypeStruct((OWN, D), F32),
            jax.ShapeDtypeStruct((D, D), BF16),
            jax.ShapeDtypeStruct((BLK, 128), F32),
        ),
        in_specs=[pl.BlockSpec(memory_space=pl.ANY)] * 7,
        out_specs=(vmem,) * 3,
        scratch_shapes=[
            pltpu.VMEM((OWN, D), BF16),
            pltpu.VMEM((BLK, 128), F32),
            pltpu.VMEM((D, D), BF16),
            pltpu.VMEM((BLK, 128), F32),
            pltpu.VMEM((1, 128), jnp.int32),
            pltpu.VMEM((1, 128), jnp.int32),
            pltpu.VMEM((8, 128), jnp.int32),
            pltpu.SemaphoreType.DMA((7,)),
            pltpu.VMEM((8, UNIT, D), BF16),
            pltpu.VMEM((NB, 4, UROWS, 128), BF16),
            pltpu.VMEM((2, GRP, D), BF16),
            pltpu.VMEM((2, D, 2 * GRP), BF16),
            pltpu.VMEM((2 * GRP, D), BF16),
            pltpu.VMEM((D, 2 * GRP), BF16),
            pltpu.VMEM((4, 16, 256), BF16),
            pltpu.VMEM((LANES, LANES), BF16),
            pltpu.VMEM((64, LANES), BF16),
            pltpu.VMEM((2, 16, 128), BF16),
            pltpu.VMEM((2, 16, 128), BF16),
            pltpu.VMEM((2 * GRP, LANES), BF16),
            pltpu.VMEM((2, 2 * GRP, D), F32),
            pltpu.VMEM((8, UNIT, D), BF16),
            pltpu.VMEM((6, UNIT, D), BF16),
            pltpu.VMEM((FLAT, 128), BF16),
            pltpu.VMEM((CHUNKS, CORE, 128), BF16),
            pltpu.VMEM((CHUNKS, CORE, 128), BF16),
            pltpu.VMEM((CHUNKS, 15, PIECE, 128), BF16),
            pltpu.VMEM((CHUNKS, 8, PIECE, 128), BF16),
            pltpu.VMEM((FLAT, 128), BF16),
            pltpu.SemaphoreType.DMA((NB, 4)),
            pltpu.SemaphoreType.DMA((NB, 4)),
            pltpu.SemaphoreType.DMA((8,)),
            pltpu.SemaphoreType.DMA((8,)),
            pltpu.SemaphoreType.DMA((N_COPIES,)),
            pltpu.SemaphoreType.DMA((N_COPIES,)),
        ],
        compiler_params=pltpu.CompilerParams(
            collective_id=0, has_side_effects=True, vmem_limit_bytes=60 * 2**20
        ),
    )(
        songs.reshape(OWN, D),
        gain.reshape(BLK, 128),
        enc_weight,
        score_vec.reshape(BLK, 128),
        left_local.reshape(1, 128),
        right_song.reshape(1, 128),
        clique.reshape(8, 128),
    )
    return (
        gf.reshape(4, FR, D),
        weight.astype(F32),
        total.reshape(D),
    )


def solution(mesh):
    in_specs = (
        P(("grp", "dev"), None, None),
        P(),
        P(),
        P(),
        P(("grp", "dev")),
        P(("grp", "dev")),
        P(),
    )
    out_specs = (P(("grp", "dev"), None, None), P(), P())
    return jax.shard_map(local, mesh=mesh, in_specs=in_specs, out_specs=out_specs, check_vma=False)
```

```python
import functools
import math

import jax
import jax.numpy as jnp
from jax import lax
from jax.experimental import pallas as pl
from jax.experimental.pallas import tpu as pltpu
from jax.sharding import PartitionSpec as P

D = 768
FR = 48
OWN = 4 * FR
GRP = 2 * OWN
UNIT = 2 * FR
BLK = D // 128
UROWS = UNIT * BLK + 16
LANES = 8 * FR
NB = 8
STEPS = 2 * NB
POLLS = ((0, 1), (2, 2), (3, 3), (4, 4), (6, 5), (8, 6), (11, 7))
ORDER = (
    (0, 0), (1, 0), (2, 0), (0, 1), (1, 1), (2, 1), (3, 0), (3, 1),
    (4, 0), (4, 1), (5, 1), (6, 1), (7, 1), (5, 0), (6, 0), (7, 0),
)
FIRST = (0, 1, 2, 6, 8, 10, 11, 12)
FOREIGN_DONE = 14
FAR = (0, 0, 1, 3, 1, 3, 2, 2)
PART = (0, 1, 1, 0, 0, 1, 0, 1)
LOSS_SCALE = 16.0
LOG2E = math.log2(math.e)
C0 = 1.0 / (math.sqrt(FR) * math.sqrt(D))
F32 = jnp.float32
BF16 = jnp.bfloat16
MESH = pl.DeviceIdType.MESH


def dot_nn(a, b):
    return jnp.dot(a, b, preferred_element_type=F32)


def dot_nt(a, b):
    return lax.dot_general(a, b, (((1,), (1,)), ((), ())), preferred_element_type=F32)


def dot_tn(a, b):
    return lax.dot_general(a, b, (((0,), (0,)), ((), ())), preferred_element_type=F32)


def col_softmax(scores):
    scale = LOG2E / math.sqrt(D)
    top = jnp.max(scores, axis=0, keepdims=True)
    e = jnp.exp2((scores - top) * scale)
    return e * (1.0 / jnp.sum(e, axis=0, keepdims=True))


def batch_scores(peer, own_t):
    st = dot_nn(peer, own_t)
    scores_x = st[:, :GRP]
    ps, gs = [], []
    for p in range(8):
        prob = col_softmax(scores_x[p * FR : (p + 1) * FR]).astype(BF16)
        pf = prob.astype(F32)
        prod = st[p * FR : (p + 1) * FR, GRP:]
        zz = pf * prod
        ps.append(prob)
        gs.append((zz - pf * jnp.sum(zz, axis=0, keepdims=True)).astype(BF16))
    by_peer = jnp.concatenate(ps, axis=0).T
    grad_peer = jnp.concatenate(gs, axis=0).T
    return by_peer, grad_peer, st.T


def batch_terms(by_peer, grad_peer, both, seg, weights, signs):
    total, first, second, z1s = [], [], [], []
    for a in range(8):
        rows = slice(a * FR, (a + 1) * FR)
        t = both[GRP + a * FR : GRP + (a + 1) * FR]
        p1 = by_peer[rows].astype(F32)
        p2 = col_softmax(both[rows]).astype(BF16).astype(F32)
        z2 = p2 * t
        r2 = jnp.sum(z2, axis=0, keepdims=True)
        total.append(jnp.sum(p1 * t, axis=0, keepdims=True) + r2)
        first.append(p1 + p2)
        second.append(z2 - p2 * r2 + grad_peer[rows].astype(F32))
    sums = jnp.concatenate(total, axis=0)
    high = sums.astype(BF16)
    low = (sums - high.astype(F32)).astype(BF16)
    spread = dot_nn(jnp.concatenate([high, low], axis=0), seg)
    logit = (spread[:8] + spread[8:]) * C0
    coef = weights * signs * (-LOSS_SCALE * C0) / (1.0 + jnp.exp(signs * logit))
    out1, out2 = [], []
    for a in range(8):
        c = coef[a : a + 1]
        out1.append((c * first[a]).astype(BF16))
        out2.append((c * second[a]).astype(BF16))
    return jnp.concatenate(out1 + out2, axis=0)


CHUNKS = 2
PIECE = 80
CORE = 16 * PIECE
CHUNK = 2 * CORE
FLAT = CHUNKS * CHUNK
WEIGHT = BLK * D
N_COPIES = 3 + 6 + CHUNKS * (1 + 15 + 7 + 15 + 1)


def kernel(
    x_hbm, gain_hbm, w_hbm, v_hbm, left_hbm, right_hbm, clique_hbm,
    gf_ref, out_ref, score_ref,
    x_ref, gain_ref, w_ref, v_ref, left_ref, right_ref, clique_ref, in_sems,
    xin, buf, own_st, own_t, hid, hid_t, cnt, seg, ind_m, sel, small, terms, acc,
    give, back, relay,
    flat, rc, half, rp, rz, full,
    csend, crecv, xsend, xrecv, sems, rems,
):
    y = lax.axis_index("grp")
    me = lax.axis_index("dev")
    core = me % 2
    chip = me // 2
    x = chip % 4
    z = chip // 4
    sib = (y, me + 1 - 2 * core)
    along_x = [(y, (z * 4 + (x + s) % 4) * 2 + core) for s in range(1, 4)]
    along_z = [(y, (((z + s) % 8) * 4 + x) * 2 + core) for s in range(1, 8)]
    spread = [(sy, sx) for sy in range(4) for sx in range(4) if sy or sx]
    plane = [((y + sy) % 4, (z * 4 + (x + sx) % 4) * 2 + core) for sy, sx in spread]
    x_up, x_far, x_down = along_x
    z_up, z_down = along_z[0], along_z[6]

    inputs = [
        pltpu.make_async_copy(src, dst, in_sems.at[n])
        for n, (src, dst) in enumerate(
            (
                (x_hbm, x_ref),
                (left_hbm, left_ref),
                (right_hbm, right_ref),
                (w_hbm, w_ref),
                (gain_hbm, gain_ref),
                (v_hbm, v_ref),
                (clique_hbm, clique_ref),
            )
        )
    ]
    for copy in inputs:
        copy.start()
    barrier = pltpu.get_barrier_semaphore()
    for dev in [sib] + plane + along_z:
        pl.semaphore_signal(barrier, inc=1, device_id=dev, device_id_type=MESH)

    def column(sb, su, db, du, dev):
        return pltpu.make_async_remote_copy(
            src_ref=buf.at[sb, su], dst_ref=buf.at[db, du],
            send_sem=csend.at[db, du], recv_sem=crecv.at[db, du],
            device_id=dev, device_id_type=MESH,
        )

    def row_unit(src, dst, dev):
        source = xin.at[src] if src > 1 else x_hbm.at[pl.ds(src * UNIT, UNIT)]
        return pltpu.make_async_remote_copy(
            src_ref=source, dst_ref=xin.at[dst],
            send_sem=xsend.at[dst], recv_sem=xrecv.at[dst],
            device_id=dev, device_id_type=MESH,
        )

    count = [0]
    pending = []

    def remote(src, dst, dev, start=True):
        i = count[0]
        count[0] += 1
        copy = pltpu.make_async_remote_copy(
            src_ref=src, dst_ref=dst, send_sem=sems.at[i], recv_sem=rems.at[i],
            device_id=dev, device_id_type=MESH,
        )
        if start:
            copy.start()
        pending.append(copy)
        return copy

    def rows(start, size):
        return pl.ds(pl.multiple_of(start, 16), size)

    def ids(shape, dim):
        return lax.broadcasted_iota(jnp.int32, shape, dim)

    def mark(cond):
        return jnp.where(cond, 1.0, 0.0).astype(BF16)

    pl.semaphore_wait(barrier, 23)
    row_unit(1, 2, x_down).start()
    row_unit(0, 3, x_up).start()
    row_unit(0, 4, x_down).start()
    row_unit(1, 5, x_up).start()
    for copy in inputs[1:3]:
        copy.wait()
    hot_left = mark(ids((16, 128), 0) == left_ref[...])
    hot_right = mark(ids((256, 128), 0) == right_ref[...] - y * 256)
    counts = dot_nt(hot_left, hot_right)
    cnt[0] = counts.astype(BF16)
    tables = [remote(cnt.at[0], cnt.at[3 - s], dev) for s, dev in enumerate(along_x)]

    for copy in inputs[:1] + inputs[3:]:
        copy.wait()

    def wide(ref):
        return jnp.concatenate([ref[j : j + 1, :] for j in range(BLK)], axis=1)

    gain = wide(gain_ref)
    score_vec = wide(v_ref)

    def encode(songs):
        values = songs.astype(F32)
        square_mean = jnp.mean(values * values, axis=-1, keepdims=True)
        hidden = (values * lax.rsqrt(square_mean + 1e-06) * gain).astype(BF16)
        feats = (values + dot_nn(hidden, w_ref[...])).astype(BF16)
        return hidden, feats

    hidden, feats = encode(x_ref[...])
    hid[:OWN] = hidden
    for k in range(2):
        for j in range(BLK):
            buf[0, k, j * UNIT : (j + 1) * UNIT, :] = feats[
                k * UNIT : (k + 1) * UNIT, j * 128 : (j + 1) * 128
            ]
        lines = [
            counts[2 * k + l : 2 * k + l + 1, h * 128 : (h + 1) * 128]
            for l in range(2)
            for h in range(2)
        ]
        buf[0, k, BLK * UNIT : UROWS, :] = jnp.concatenate(
            lines + [jnp.zeros((12, 128), F32)], axis=0
        ).astype(BF16)
    for k in range(2):
        column(0, k, 1 + k, 0, z_up).start()
        column(0, k, 1 + k, 1, z_down).start()
        column(0, k, 0, 2 + k, sib).start()

    lane_song = ids((1, LANES), 1) // FR
    for a in range(8):
        seg[a * FR : (a + 1) * FR] = mark(ids((FR, LANES), 0) * 0 + lane_song == a)
    row = ids((64, 1), 0)
    song = 2 * (row // 16) + (row % 16) // 2
    song = jnp.where(jnp.logical_and(row % 16 < 4, row % 2 == z // 4), song, -1)
    ind_m[...] = mark(song == lane_song)
    acc[...] = jnp.zeros_like(acc)
    terms[...] = jnp.zeros_like(terms)

    lane = ids((1, 128), 1)
    b = lane // 8
    u = (lane % 8) // 2
    way = u % 2
    t = (b + 1) // 2
    dz = jnp.where(b == 0, 0, jnp.where(way == 0, 8 - t % 8, t))
    k = jnp.where(jnp.logical_or(b == 0, b == NB - 1), way, (b + 1) % 2)
    held = (((z + dz) % 8) * 4 + x) * 2 + jnp.where(u < 2, core, 1 - core)
    landing = held * 4 + 2 * k + lane % 2
    hot = mark(ids((256, 128), 0) == landing)
    group_rows = [clique_ref[pl.ds(2 * y + h, 1), :] for h in range(2)]
    theirs = jnp.concatenate(group_rows, axis=1).astype(F32)
    near_row = clique_ref[pl.ds(2 * y + z // 4, 1), :].astype(F32)
    for copy in tables:
        copy.wait_recv()
    for r in range(2):
        shape = (16, 128)
        row = ids(shape, 0)
        number = row * 0 - 1
        for w in range(4):
            first = ((z % 4) * 4 + (x + FAR[4 * r + w]) % 4) * 8 + core * 4 + 2 * PART[4 * r + w]
            number = jnp.where(row // 2 == w, first + row % 2, number)
        chosen = ids(shape, 1) == number
        sel[r] = mark(chosen)
        mine = jnp.sum(jnp.where(chosen, near_row, 0.0), axis=1, keepdims=True)[:8]
        signs = jnp.where(mine == theirs, 1.0, -1.0)
        left = [
            cnt[FAR[4 * r + w]].astype(F32)[2 * PART[4 * r + w] : 2 * PART[4 * r + w] + 2]
            for w in range(4)
        ]
        table = jnp.concatenate(left + [signs], axis=0).astype(BF16)
        small[r] = dot_nn(table, hot).astype(BF16)

    def prepare(r, start, feats):
        size = feats.shape[0]
        scaled = (feats.astype(F32) * score_vec).astype(BF16)
        own_st[r, start : start + size] = feats
        own_t[r, :, start : start + size] = feats.T
        own_t[r, :, GRP + start : GRP + start + size] = scaled.T

    def arrived(b, u):
        column(b, u, b, u, sib).wait_recv()

    prepare(0, 0, feats)
    for u in (2, 3):
        row_unit(u, u, x_up).wait_recv()
    row_unit(3, 6, x_up).start()
    row_unit(2, 7, x_down).start()
    hidden, feats = encode(xin[2:4].reshape(OWN, D))
    hid[OWN:GRP] = hidden
    prepare(0, OWN, feats)

    def peer_of(b):
        return jnp.concatenate(
            [
                buf[b, :, j * UNIT : (j + 1) * UNIT, :].reshape(LANES, 128)
                for j in range(BLK)
            ],
            axis=1,
        )

    def order(i):
        code = i * 0
        for n, (b, r) in enumerate(ORDER):
            code = jnp.where(i == n, 2 * b + r, code)
        return code // 2, code % 2

    def gradients(r):
        first = acc[r, :GRP]
        grads = score_vec * first + acc[r, GRP:] * (1.0 / math.sqrt(D))
        give[4 * r : 4 * r + 4] = grads.astype(BF16).reshape(4, UNIT, D)
        return first, grads

    relays = [
        remote(give.at[6], relay.at[0], x_up, start=False),
        remote(give.at[7], relay.at[1], x_down, start=False),
    ]

    def step(i, carry):
        b, r = order(i)

        for at, ahead in POLLS:

            @pl.when(i == at)
            def _():
                for way, dev in ((0, z_up), (1, z_down)):
                    arrived(ahead, way)
                    if ahead < 5:
                        column(ahead, way, ahead + 2, way, dev).start()
                    elif ahead == 5 + way:
                        column(ahead, way, 7, way, dev).start()
                    column(ahead, way, ahead, 2 + way, sib).start()

        @pl.when(i == 3)
        def _():
            for u in (4, 5, 6, 7):
                row_unit(u, u, x_up).wait_recv()
            hidden, feats = encode(xin[4:8].reshape(GRP, D))
            hid[GRP:] = hidden
            prepare(1, 0, feats)
            hid_t[...] = hid[...].T

        @pl.when(i == FOREIGN_DONE)
        def _():
            gradients(1)
            for copy in relays:
                copy.start()

        fresh = i == FIRST[0]
        for n in FIRST[1:]:
            fresh = jnp.logical_or(fresh, i == n)

        @pl.when(fresh)
        def _():
            for k in range(2):
                arrived(b, 2 + k)

        peer = peer_of(b)
        by_peer, grad_peer, both = batch_scores(peer, own_t[r])

        before, rows_before = order(jnp.maximum(i - 1, 0))
        acc[rows_before] += dot_nn(terms[...], peer_of(before))
        meta = buf[b, :, BLK * UNIT : UROWS, :].reshape(64, 128)
        wexp = dot_nn(small[r], mark(ids((128, LANES), 0) == lane_song + 8 * b))
        right = dot_nn(dot_nt(sel[r], meta).astype(BF16), ind_m[...])
        terms[...] = batch_terms(
            by_peer, grad_peer, both, seg[...], wexp[:8] + right[:8], wexp[8:]
        )
        return carry

    lax.fori_loop(0, STEPS, step, 0)
    acc[0] += dot_nn(terms[...], peer_of(NB - 1))
    first, grads = gradients(0)
    gf_ref[...] = grads[:OWN]
    score = 0.5 * jnp.sum(
        own_st[0].astype(F32) * first + own_st[1].astype(F32) * acc[1, :GRP],
        axis=0,
        keepdims=True,
    )
    for j in range(BLK):
        high = give[:, :, j * 128 : (j + 1) * 128].reshape(2 * GRP, 128)
        flat[j * D : (j + 1) * D, :] = dot_nn(hid_t[...], high).astype(BF16)
    flat[WEIGHT : WEIGHT + 16, :] = jnp.concatenate(
        [score[:, j * 128 : (j + 1) * 128] for j in range(BLK)]
        + [jnp.zeros((16 - BLK, 128), F32)],
        axis=0,
    ).astype(BF16)
    flat[WEIGHT + 16 :, :] = jnp.zeros((FLAT - WEIGHT - 16, 128), BF16)

    chunks = range(CHUNKS)
    copies = [
        remote(flat.at[rows(h * CHUNK + (1 - core) * CORE, CORE)], rc.at[h], sib)
        for h in chunks
    ]
    plane_copies = []
    for h in chunks:
        copies[h].wait_recv()
        half[h] = (
            flat[rows(h * CHUNK + core * CORE, CORE), :].astype(F32) + rc[h].astype(F32)
        ).astype(BF16)
        plane_copies.append(
            [
                remote(
                    half.at[h, rows((((y + sy) % 4) * 4 + (x + sx) % 4) * PIECE, PIECE)],
                    rp.at[h, n],
                    plane[n],
                )
                for n, (sy, sx) in enumerate(spread)
            ]
        )
    returned = [remote(give.at[2], back.at[1], x_up), remote(give.at[3], back.at[2], x_down)]
    for n, slot, dev in ((0, 0, x_up), (1, 3, x_down)):
        relays[n].wait_recv()
        relay[n] = (relay[n].astype(F32) + give[4 + n].astype(F32)).astype(BF16)
        returned.append(remote(relay.at[n], back.at[slot], dev))
    line_copies = []
    for h in chunks:
        for c in plane_copies[h]:
            c.wait_recv()
        total = half[h, rows((y * 4 + x) * PIECE, PIECE), :].astype(F32)
        for n in range(15):
            total = total + rp[h, n].astype(F32)
        rz[h, z] = total.astype(BF16)
        line_copies.append([remote(rz.at[h, z], rz.at[h, z], dev) for dev in along_z])
    plane_copies = []
    for h in chunks:
        for c in line_copies[h]:
            c.wait_recv()
        total = rz[h, 0].astype(F32)
        for n in range(1, 8):
            total = total + rz[h, n].astype(F32)
        mine = rows(h * CHUNK + core * CORE + (y * 4 + x) * PIECE, PIECE)
        full[mine, :] = total.astype(BF16)
        plane_copies.append([remote(full.at[mine], full.at[mine], dev) for dev in plane])
    copies = []
    for h in chunks:
        for c in plane_copies[h]:
            c.wait_recv()
        same = rows(h * CHUNK + core * CORE, CORE)
        copies.append(remote(full.at[same], full.at[same], sib))
    for copy in returned:
        copy.wait_recv()
    for k in range(2):
        part = slice(k * UNIT, (k + 1) * UNIT)
        gf_ref[part, :] = (
            (gf_ref[part, :] + back[k].astype(F32))
            + back[2 + k].astype(F32)
        )
    for c in copies:
        c.wait_recv()
    for j in range(BLK):
        out_ref[:, j * 128 : (j + 1) * 128] = full[j * D : (j + 1) * D, :]
    score_ref[...] = full[WEIGHT : WEIGHT + 16, :].astype(F32)[:BLK]
    for c in pending:
        c.wait_send()
    for u in range(2, 8):
        row_unit(u, u, x_up).wait_send()
    for b in range(NB):
        for u in range(4):
            if b or u > 1:
                column(b, u, b, u, sib).wait_send()


def local(songs, gain, enc_weight, score_vec, left_local, right_song, clique):
    vmem = pl.BlockSpec(memory_space=pltpu.VMEM)
    gf, weight, total = pl.pallas_call(
        kernel,
        out_shape=(
            jax.ShapeDtypeStruct((OWN, D), F32),
            jax.ShapeDtypeStruct((D, D), BF16),
            jax.ShapeDtypeStruct((BLK, 128), F32),
        ),
        in_specs=[pl.BlockSpec(memory_space=pltpu.HBM)] * 7,
        out_specs=(vmem,) * 3,
        scratch_shapes=[
            pltpu.VMEM((OWN, D), BF16),
            pltpu.VMEM((BLK, 128), F32),
            pltpu.VMEM((D, D), BF16),
            pltpu.VMEM((BLK, 128), F32),
            pltpu.VMEM((1, 128), jnp.int32),
            pltpu.VMEM((1, 128), jnp.int32),
            pltpu.VMEM((8, 128), jnp.int32),
            pltpu.SemaphoreType.DMA((7,)),
            pltpu.VMEM((8, UNIT, D), BF16),
            pltpu.VMEM((NB, 4, UROWS, 128), BF16),
            pltpu.VMEM((2, GRP, D), BF16),
            pltpu.VMEM((2, D, 2 * GRP), BF16),
            pltpu.VMEM((2 * GRP, D), BF16),
            pltpu.VMEM((D, 2 * GRP), BF16),
            pltpu.VMEM((4, 16, 256), BF16),
            pltpu.VMEM((LANES, LANES), BF16),
            pltpu.VMEM((64, LANES), BF16),
            pltpu.VMEM((2, 16, 128), BF16),
            pltpu.VMEM((2, 16, 128), BF16),
            pltpu.VMEM((2 * GRP, LANES), BF16),
            pltpu.VMEM((2, 2 * GRP, D), F32),
            pltpu.VMEM((8, UNIT, D), BF16),
            pltpu.VMEM((4, UNIT, D), BF16),
            pltpu.VMEM((2, UNIT, D), BF16),
            pltpu.VMEM((FLAT, 128), BF16),
            pltpu.VMEM((CHUNKS, CORE, 128), BF16),
            pltpu.VMEM((CHUNKS, CORE, 128), BF16),
            pltpu.VMEM((CHUNKS, 15, PIECE, 128), BF16),
            pltpu.VMEM((CHUNKS, 8, PIECE, 128), BF16),
            pltpu.VMEM((FLAT, 128), BF16),
            pltpu.SemaphoreType.DMA((NB, 4)),
            pltpu.SemaphoreType.DMA((NB, 4)),
            pltpu.SemaphoreType.DMA((8,)),
            pltpu.SemaphoreType.DMA((8,)),
            pltpu.SemaphoreType.DMA((N_COPIES,)),
            pltpu.SemaphoreType.DMA((N_COPIES,)),
        ],
        compiler_params=pltpu.CompilerParams(
            collective_id=0, has_side_effects=True, vmem_limit_bytes=60 * 2**20
        ),
    )(
        songs.reshape(OWN, D),
        gain.reshape(BLK, 128),
        enc_weight,
        score_vec.reshape(BLK, 128),
        left_local.reshape(1, 128),
        right_song.reshape(1, 128),
        clique.reshape(8, 128),
    )
    return (
        gf.reshape(4, FR, D),
        weight.astype(F32),
        total.reshape(D),
    )


def solution(mesh):
    in_specs = (
        P(("grp", "dev"), None, None),
        P(),
        P(),
        P(),
        P(("grp", "dev")),
        P(("grp", "dev")),
        P(),
    )
    out_specs = (P(("grp", "dev"), None, None), P(), P())
    return jax.shard_map(local, mesh=mesh, in_specs=in_specs, out_specs=out_specs, check_vma=False)
```

```python
import functools
import math

import jax
import jax.numpy as jnp
from jax import lax
from jax.experimental import pallas as pl
from jax.experimental.pallas import tpu as pltpu
from jax.sharding import PartitionSpec as P

D = 768
FR = 48
OWN = 4 * FR
GRP = 2 * OWN
UNIT = 2 * FR
BLK = D // 128
UROWS = UNIT * BLK + 16
LANES = 8 * FR
NB = 8
STEPS = 2 * NB
POLLS = ((0, 1), (2, 2), (3, 3), (4, 4), (6, 5), (8, 6), (11, 7))
ORDER = (
    (0, 0), (1, 0), (2, 0), (0, 1), (1, 1), (2, 1), (3, 0), (3, 1),
    (4, 0), (4, 1), (5, 1), (6, 1), (7, 1), (5, 0), (6, 0), (7, 0),
)
FIRST = (0, 1, 2, 6, 8, 10, 11, 12)
FOREIGN_DONE = 14
FAR = (0, 0, 1, 3, 1, 3, 2, 2)
PART = (0, 1, 1, 0, 0, 1, 0, 1)
LOSS_SCALE = 16.0
LOG2E = math.log2(math.e)
C0 = 1.0 / (math.sqrt(FR) * math.sqrt(D))
F32 = jnp.float32
BF16 = jnp.bfloat16
MESH = pl.DeviceIdType.MESH


def dot_nn(a, b):
    return jnp.dot(a, b, preferred_element_type=F32)


def dot_nt(a, b):
    return lax.dot_general(a, b, (((1,), (1,)), ((), ())), preferred_element_type=F32)


def dot_tn(a, b):
    return lax.dot_general(a, b, (((0,), (0,)), ((), ())), preferred_element_type=F32)


def col_softmax(scores):
    scale = LOG2E / math.sqrt(D)
    top = jnp.max(scores, axis=0, keepdims=True)
    e = jnp.exp2((scores - top) * scale)
    return e * (1.0 / jnp.sum(e, axis=0, keepdims=True))


def batch_scores(peer, own_t):
    st = dot_nn(peer, own_t)
    scores_x = st[:, :GRP]
    ps, gs = [], []
    for p in range(8):
        prob = col_softmax(scores_x[p * FR : (p + 1) * FR]).astype(BF16)
        pf = prob.astype(F32)
        prod = st[p * FR : (p + 1) * FR, GRP:]
        zz = pf * prod
        ps.append(prob)
        gs.append((zz - pf * jnp.sum(zz, axis=0, keepdims=True)).astype(BF16))
    by_peer = jnp.concatenate(ps, axis=0).T
    grad_peer = jnp.concatenate(gs, axis=0).T
    return by_peer, grad_peer, st.T


def batch_terms(by_peer, grad_peer, both, seg, weights, signs):
    total, first, second, z1s = [], [], [], []
    for a in range(8):
        rows = slice(a * FR, (a + 1) * FR)
        t = both[GRP + a * FR : GRP + (a + 1) * FR]
        p1 = by_peer[rows].astype(F32)
        p2 = col_softmax(both[rows]).astype(BF16).astype(F32)
        z2 = p2 * t
        r2 = jnp.sum(z2, axis=0, keepdims=True)
        total.append(jnp.sum(p1 * t, axis=0, keepdims=True) + r2)
        first.append(p1 + p2)
        second.append(z2 - p2 * r2 + grad_peer[rows].astype(F32))
    sums = jnp.concatenate(total, axis=0)
    high = sums.astype(BF16)
    low = (sums - high.astype(F32)).astype(BF16)
    spread = dot_nn(jnp.concatenate([high, low], axis=0), seg)
    logit = (spread[:8] + spread[8:]) * C0
    coef = weights * signs * (-LOSS_SCALE * C0) / (1.0 + jnp.exp(signs * logit))
    out1, out2 = [], []
    for a in range(8):
        c = coef[a : a + 1]
        out1.append((c * first[a]).astype(BF16))
        out2.append((c * second[a]).astype(BF16))
    return jnp.concatenate(out1 + out2, axis=0)


CHUNKS = 2
PIECE = 80
CORE = 16 * PIECE
CHUNK = 2 * CORE
FLAT = CHUNKS * CHUNK
WEIGHT = BLK * D
N_COPIES = 3 + 6 + CHUNKS * (1 + 15 + 7 + 15 + 4)


def kernel(
    x_hbm, gain_hbm, w_hbm, v_hbm, left_hbm, right_hbm, clique_hbm,
    gf_ref, out_ref, score_ref,
    x_ref, gain_ref, w_ref, v_ref, left_ref, right_ref, clique_ref, in_sems,
    xin, buf, own_st, own_t, hid, hid_t, cnt, seg, ind_m, sel, tab, terms, acc,
    give, back, relay,
    flat, rc, half, rp, rz, full,
    csend, crecv, xsend, xrecv, sems, rems,
):
    y = lax.axis_index("grp")
    me = lax.axis_index("dev")
    core = me % 2
    chip = me // 2
    x = chip % 4
    z = chip // 4
    sib = (y, me + 1 - 2 * core)
    along_x = [(y, (z * 4 + (x + s) % 4) * 2 + core) for s in range(1, 4)]
    along_z = [(y, (((z + s) % 8) * 4 + x) * 2 + core) for s in range(1, 8)]
    spread = [(sy, sx) for sy in range(4) for sx in range(4) if sy or sx]
    plane = [((y + sy) % 4, (z * 4 + (x + sx) % 4) * 2 + core) for sy, sx in spread]
    x_up, x_far, x_down = along_x
    z_up, z_down = along_z[0], along_z[6]

    inputs = [
        pltpu.make_async_copy(src, dst, in_sems.at[n])
        for n, (src, dst) in enumerate(
            (
                (x_hbm, x_ref),
                (left_hbm, left_ref),
                (right_hbm, right_ref),
                (w_hbm, w_ref),
                (gain_hbm, gain_ref),
                (v_hbm, v_ref),
                (clique_hbm, clique_ref),
            )
        )
    ]
    for copy in inputs:
        copy.start()
    barrier = pltpu.get_barrier_semaphore()
    for dev in [sib] + plane + along_z:
        pl.semaphore_signal(barrier, inc=1, device_id=dev, device_id_type=MESH)

    def column(sb, su, db, du, dev):
        return pltpu.make_async_remote_copy(
            src_ref=buf.at[sb, su], dst_ref=buf.at[db, du],
            send_sem=csend.at[db, du], recv_sem=crecv.at[db, du],
            device_id=dev, device_id_type=MESH,
        )

    def row_unit(src, dst, dev):
        source = xin.at[src] if src > 1 else x_hbm.at[pl.ds(src * UNIT, UNIT)]
        return pltpu.make_async_remote_copy(
            src_ref=source, dst_ref=xin.at[dst],
            send_sem=xsend.at[dst], recv_sem=xrecv.at[dst],
            device_id=dev, device_id_type=MESH,
        )

    count = [0]
    pending = []

    def remote(src, dst, dev, start=True):
        i = count[0]
        count[0] += 1
        copy = pltpu.make_async_remote_copy(
            src_ref=src, dst_ref=dst, send_sem=sems.at[i], recv_sem=rems.at[i],
            device_id=dev, device_id_type=MESH,
        )
        if start:
            copy.start()
        pending.append(copy)
        return copy

    def rows(start, size):
        return pl.ds(pl.multiple_of(start, 16), size)

    def ids(shape, dim):
        return lax.broadcasted_iota(jnp.int32, shape, dim)

    def mark(cond):
        return jnp.where(cond, 1.0, 0.0).astype(BF16)

    pl.semaphore_wait(barrier, 23)
    row_unit(1, 2, x_down).start()
    row_unit(0, 3, x_up).start()
    row_unit(0, 4, x_down).start()
    row_unit(1, 5, x_up).start()
    for copy in inputs[1:3]:
        copy.wait()
    hot_left = mark(ids((16, 128), 0) == left_ref[...])
    hot_right = mark(ids((256, 128), 0) == right_ref[...] - y * 256)
    counts = dot_nt(hot_left, hot_right)
    cnt[0] = counts.astype(BF16)
    tables = [remote(cnt.at[0], cnt.at[3 - s], dev) for s, dev in enumerate(along_x)]

    for copy in inputs[:1] + inputs[3:]:
        copy.wait()

    def wide(ref):
        return jnp.concatenate([ref[j : j + 1, :] for j in range(BLK)], axis=1)

    gain = wide(gain_ref)
    score_vec = wide(v_ref)

    def encode(songs):
        values = songs.astype(F32)
        square_mean = jnp.mean(values * values, axis=-1, keepdims=True)
        hidden = (values * lax.rsqrt(square_mean + 1e-06) * gain).astype(BF16)
        feats = (values + dot_nn(hidden, w_ref[...])).astype(BF16)
        return hidden, feats

    hidden, feats = encode(x_ref[...])
    hid[:OWN] = hidden
    for k in range(2):
        for j in range(BLK):
            buf[0, k, j * UNIT : (j + 1) * UNIT, :] = feats[
                k * UNIT : (k + 1) * UNIT, j * 128 : (j + 1) * 128
            ]
        lines = [
            counts[2 * k + l : 2 * k + l + 1, h * 128 : (h + 1) * 128]
            for l in range(2)
            for h in range(2)
        ]
        buf[0, k, BLK * UNIT : UROWS, :] = jnp.concatenate(
            lines + [jnp.zeros((12, 128), F32)], axis=0
        ).astype(BF16)
    for k in range(2):
        column(0, k, 1 + k, 0, z_up).start()
        column(0, k, 1 + k, 1, z_down).start()
        column(0, k, 0, 2 + k, sib).start()

    lane_song = ids((1, LANES), 1) // FR
    for a in range(8):
        seg[a * FR : (a + 1) * FR] = mark(ids((FR, LANES), 0) * 0 + lane_song == a)
    row = ids((64, 1), 0)
    song = 2 * (row // 16) + (row % 16) // 2
    song = jnp.where(jnp.logical_and(row % 16 < 4, row % 2 == z // 4), song, -1)
    ind_m[...] = mark(song == lane_song)
    acc[...] = jnp.zeros_like(acc)
    terms[...] = jnp.zeros_like(terms)

    lane = ids((1, 128), 1)
    b = lane // 8
    u = (lane % 8) // 2
    way = u % 2
    t = (b + 1) // 2
    dz = jnp.where(b == 0, 0, jnp.where(way == 0, 8 - t % 8, t))
    k = jnp.where(jnp.logical_or(b == 0, b == NB - 1), way, (b + 1) % 2)
    held = (((z + dz) % 8) * 4 + x) * 2 + jnp.where(u < 2, core, 1 - core)
    landing = held * 4 + 2 * k + lane % 2
    hot = mark(ids((256, 128), 0) == landing)
    group_rows = [clique_ref[pl.ds(2 * y + h, 1), :] for h in range(2)]
    theirs = jnp.concatenate(group_rows, axis=1).astype(F32)
    near_row = clique_ref[pl.ds(2 * y + z // 4, 1), :].astype(F32)
    for copy in tables:
        copy.wait_recv()
    for r in range(2):
        shape = (16, 128)
        row = ids(shape, 0)
        number = row * 0 - 1
        for w in range(4):
            first = ((z % 4) * 4 + (x + FAR[4 * r + w]) % 4) * 8 + core * 4 + 2 * PART[4 * r + w]
            number = jnp.where(row // 2 == w, first + row % 2, number)
        chosen = ids(shape, 1) == number
        sel[r] = mark(chosen)
        mine = jnp.sum(jnp.where(chosen, near_row, 0.0), axis=1, keepdims=True)[:8]
        signs = jnp.where(mine == theirs, 1.0, -1.0)
        left = [
            cnt[FAR[4 * r + w]].astype(F32)[2 * PART[4 * r + w] : 2 * PART[4 * r + w] + 2]
            for w in range(4)
        ]
        table = jnp.concatenate(left + [signs], axis=0).astype(BF16)
        small = dot_nn(table, hot).astype(BF16)
        for b in range(NB):
            tab[r, b] = dot_nn(small, mark(ids((128, LANES), 0) == lane_song + 8 * b))

    def prepare(r, start, feats):
        size = feats.shape[0]
        scaled = (feats.astype(F32) * score_vec).astype(BF16)
        own_st[r, start : start + size] = feats
        own_t[r, :, start : start + size] = feats.T
        own_t[r, :, GRP + start : GRP + start + size] = scaled.T

    def arrived(b, u):
        column(b, u, b, u, sib).wait_recv()

    prepare(0, 0, feats)
    for u in (2, 3):
        row_unit(u, u, x_up).wait_recv()
    row_unit(3, 6, x_up).start()
    row_unit(2, 7, x_down).start()
    hidden, feats = encode(xin[2:4].reshape(OWN, D))
    hid[OWN:GRP] = hidden
    prepare(0, OWN, feats)

    def peer_of(b):
        return jnp.concatenate(
            [
                buf[b, :, j * UNIT : (j + 1) * UNIT, :].reshape(LANES, 128)
                for j in range(BLK)
            ],
            axis=1,
        )

    def order(i):
        code = i * 0
        for n, (b, r) in enumerate(ORDER):
            code = jnp.where(i == n, 2 * b + r, code)
        return code // 2, code % 2

    def gradients(r):
        first = acc[r, :GRP]
        grads = score_vec * first + acc[r, GRP:] * (1.0 / math.sqrt(D))
        give[4 * r : 4 * r + 4] = grads.astype(BF16).reshape(4, UNIT, D)
        return first, grads

    relays = [
        remote(give.at[6], relay.at[0], x_up, start=False),
        remote(give.at[7], relay.at[1], x_down, start=False),
    ]

    def step(i, carry):
        b, r = order(i)

        for at, ahead in POLLS:

            @pl.when(i == at)
            def _():
                for way, dev in ((0, z_up), (1, z_down)):
                    arrived(ahead, way)
                    if ahead < 5:
                        column(ahead, way, ahead + 2, way, dev).start()
                    elif ahead == 5 + way:
                        column(ahead, way, 7, way, dev).start()
                    column(ahead, way, ahead, 2 + way, sib).start()

        @pl.when(i == 3)
        def _():
            for u in (4, 5, 6, 7):
                row_unit(u, u, x_up).wait_recv()
            hidden, feats = encode(xin[4:8].reshape(GRP, D))
            hid[GRP:] = hidden
            prepare(1, 0, feats)
            hid_t[...] = hid[...].T

        @pl.when(i == FOREIGN_DONE)
        def _():
            gradients(1)
            for copy in relays:
                copy.start()

        fresh = i == FIRST[0]
        for n in FIRST[1:]:
            fresh = jnp.logical_or(fresh, i == n)

        @pl.when(fresh)
        def _():
            for k in range(2):
                arrived(b, 2 + k)

        peer = peer_of(b)
        by_peer, grad_peer, both = batch_scores(peer, own_t[r])

        before, rows_before = order(jnp.maximum(i - 1, 0))
        acc[rows_before] += dot_nn(terms[...], peer_of(before))
        meta = buf[b, :, BLK * UNIT : UROWS, :].reshape(64, 128)
        wexp = tab[r, b]
        right = dot_nn(dot_nt(sel[r], meta).astype(BF16), ind_m[...])
        terms[...] = batch_terms(
            by_peer, grad_peer, both, seg[...], wexp[:8] + right[:8], wexp[8:]
        )
        return carry

    lax.fori_loop(0, STEPS, step, 0)
    acc[0] += dot_nn(terms[...], peer_of(NB - 1))
    first, grads = gradients(0)
    gf_ref[...] = grads[:OWN]
    score = 0.5 * jnp.sum(
        own_st[0].astype(F32) * first + own_st[1].astype(F32) * acc[1, :GRP],
        axis=0,
        keepdims=True,
    )
    for j in range(BLK):
        high = give[:, :, j * 128 : (j + 1) * 128].reshape(2 * GRP, 128)
        flat[j * D : (j + 1) * D, :] = dot_nn(hid_t[...], high).astype(BF16)
    flat[WEIGHT : WEIGHT + 16, :] = jnp.concatenate(
        [score[:, j * 128 : (j + 1) * 128] for j in range(BLK)]
        + [jnp.zeros((16 - BLK, 128), F32)],
        axis=0,
    ).astype(BF16)
    flat[WEIGHT + 16 :, :] = jnp.zeros((FLAT - WEIGHT - 16, 128), BF16)

    chunks = range(CHUNKS)
    copies = [
        remote(flat.at[rows(h * CHUNK + (1 - core) * CORE, CORE)], rc.at[h], sib)
        for h in chunks
    ]
    plane_copies = []
    for h in chunks:
        copies[h].wait_recv()
        half[h] = (
            flat[rows(h * CHUNK + core * CORE, CORE), :].astype(F32) + rc[h].astype(F32)
        ).astype(BF16)
        plane_copies.append(
            [
                remote(
                    half.at[h, rows((((y + sy) % 4) * 4 + (x + sx) % 4) * PIECE, PIECE)],
                    rp.at[h, n],
                    plane[n],
                )
                for n, (sy, sx) in enumerate(spread)
            ]
        )
    returned = [remote(give.at[2], back.at[1], x_up), remote(give.at[3], back.at[2], x_down)]
    for n, slot, dev in ((0, 0, x_up), (1, 3, x_down)):
        relays[n].wait_recv()
        relay[n] = (relay[n].astype(F32) + give[4 + n].astype(F32)).astype(BF16)
        returned.append(remote(relay.at[n], back.at[slot], dev))
    line_copies = []
    for h in chunks:
        for c in plane_copies[h]:
            c.wait_recv()
        total = half[h, rows((y * 4 + x) * PIECE, PIECE), :].astype(F32)
        for n in range(15):
            total = total + rp[h, n].astype(F32)
        rz[h, z] = total.astype(BF16)
        line_copies.append([remote(rz.at[h, z], rz.at[h, z], dev) for dev in along_z])
    plane_copies = []
    for h in chunks:
        for c in line_copies[h]:
            c.wait_recv()
        total = rz[h, 0].astype(F32)
        for n in range(1, 8):
            total = total + rz[h, n].astype(F32)
        mine = rows(h * CHUNK + core * CORE + (y * 4 + x) * PIECE, PIECE)
        full[mine, :] = total.astype(BF16)
        plane_copies.append([remote(full.at[mine], full.at[mine], dev) for dev in plane])
    copies = []
    for h in chunks:
        quarters = []
        for back_y in range(4):
            for n, (sy, _) in enumerate(spread):
                if sy == back_y:
                    plane_copies[h][n].wait_recv()
            at = h * CHUNK + core * CORE + (y + 4 - back_y) % 4 * (4 * PIECE)
            same = rows(at, 4 * PIECE)
            quarters.append(remote(full.at[same], full.at[same], sib))
        copies.append(quarters)
    for copy in returned:
        copy.wait_recv()
    for k in range(2):
        part = slice(k * UNIT, (k + 1) * UNIT)
        gf_ref[part, :] = (
            (gf_ref[part, :] + back[k].astype(F32))
            + back[2 + k].astype(F32)
        )
    for h in chunks:
        for c in copies[h]:
            c.wait_recv()
        for j in range(h * BLK // 2, (h + 1) * BLK // 2):
            out_ref[:, j * 128 : (j + 1) * 128] = full[j * D : (j + 1) * D, :]
    score_ref[...] = full[WEIGHT : WEIGHT + 16, :].astype(F32)[:BLK]
    for c in pending:
        c.wait_send()
    for u in range(2, 8):
        row_unit(u, u, x_up).wait_send()
    for b in range(NB):
        for u in range(4):
            if b or u > 1:
                column(b, u, b, u, sib).wait_send()


def local(songs, gain, enc_weight, score_vec, left_local, right_song, clique):
    vmem = pl.BlockSpec(memory_space=pltpu.VMEM)
    gf, weight, total = pl.pallas_call(
        kernel,
        out_shape=(
            jax.ShapeDtypeStruct((OWN, D), F32),
            jax.ShapeDtypeStruct((D, D), BF16),
            jax.ShapeDtypeStruct((BLK, 128), F32),
        ),
        in_specs=[pl.BlockSpec(memory_space=pltpu.HBM)] * 7,
        out_specs=(vmem,) * 3,
        scratch_shapes=[
            pltpu.VMEM((OWN, D), BF16),
            pltpu.VMEM((BLK, 128), F32),
            pltpu.VMEM((D, D), BF16),
            pltpu.VMEM((BLK, 128), F32),
            pltpu.VMEM((1, 128), jnp.int32),
            pltpu.VMEM((1, 128), jnp.int32),
            pltpu.VMEM((8, 128), jnp.int32),
            pltpu.SemaphoreType.DMA((7,)),
            pltpu.VMEM((8, UNIT, D), BF16),
            pltpu.VMEM((NB, 4, UROWS, 128), BF16),
            pltpu.VMEM((2, GRP, D), BF16),
            pltpu.VMEM((2, D, 2 * GRP), BF16),
            pltpu.VMEM((2 * GRP, D), BF16),
            pltpu.VMEM((D, 2 * GRP), BF16),
            pltpu.VMEM((4, 16, 256), BF16),
            pltpu.VMEM((LANES, LANES), BF16),
            pltpu.VMEM((64, LANES), BF16),
            pltpu.VMEM((2, 16, 128), BF16),
            pltpu.VMEM((2, NB, 16, LANES), F32),
            pltpu.VMEM((2 * GRP, LANES), BF16),
            pltpu.VMEM((2, 2 * GRP, D), F32),
            pltpu.VMEM((8, UNIT, D), BF16),
            pltpu.VMEM((4, UNIT, D), BF16),
            pltpu.VMEM((2, UNIT, D), BF16),
            pltpu.VMEM((FLAT, 128), BF16),
            pltpu.VMEM((CHUNKS, CORE, 128), BF16),
            pltpu.VMEM((CHUNKS, CORE, 128), BF16),
            pltpu.VMEM((CHUNKS, 15, PIECE, 128), BF16),
            pltpu.VMEM((CHUNKS, 8, PIECE, 128), BF16),
            pltpu.VMEM((FLAT, 128), BF16),
            pltpu.SemaphoreType.DMA((NB, 4)),
            pltpu.SemaphoreType.DMA((NB, 4)),
            pltpu.SemaphoreType.DMA((8,)),
            pltpu.SemaphoreType.DMA((8,)),
            pltpu.SemaphoreType.DMA((N_COPIES,)),
            pltpu.SemaphoreType.DMA((N_COPIES,)),
        ],
        compiler_params=pltpu.CompilerParams(
            collective_id=0, has_side_effects=True, vmem_limit_bytes=60 * 2**20
        ),
    )(
        songs.reshape(OWN, D),
        gain.reshape(BLK, 128),
        enc_weight,
        score_vec.reshape(BLK, 128),
        left_local.reshape(1, 128),
        right_song.reshape(1, 128),
        clique.reshape(8, 128),
    )
    return (
        gf.reshape(4, FR, D),
        weight.astype(F32),
        total.reshape(D),
    )


def solution(mesh):
    in_specs = (
        P(("grp", "dev"), None, None),
        P(),
        P(),
        P(),
        P(("grp", "dev")),
        P(("grp", "dev")),
        P(),
    )
    out_specs = (P(("grp", "dev"), None, None), P(), P())
    return jax.shard_map(local, mesh=mesh, in_specs=in_specs, out_specs=out_specs, check_vma=False)
```
